256 devices in a mesh: panel: 16 (over z_hi, y, core), front: 16 (over z_lo, x).
Axes of the slice: x: 4, y: 4, z: 8 (z_hi: 2, z_lo: 4; z = z_hi * 4 + z_lo), core: 2. Of those that a mesh axis runs over, the one named last changes fastest.
Arguments:
- source_leaf: float32 [16, 32, 32, 1024], P('panel', 'front'), may hold values from -6 to 6
- source_sep: float32 [16, 32, 4096], P('panel', None, 'front'), may hold values from -6 to 6
- leaf_inverse: bfloat16 [16, 32, 1024, 1024], P('panel', 'front'), as said below
- lift: bfloat16 [16, 32, 1024, 512], P('panel', 'front'), may hold values from -0.1875 to 0.1875
- lower: bfloat16 [16, 32, 512, 1024], P('panel', 'front'), may hold values from -0.25 to 0.25
- sep_inverse: bfloat16 [16, 4096, 4096], P('panel', None, 'front'), as said below
- parent_map: int32 [16, 32, 512], P('panel', 'front'), may hold values from 0 to 4095, as said below
- couple_down: float32 [16, 32, 1024], P('panel', 'front'), may hold values from 0.6 to 1.2
- couple_up: float32 [16, 32, 1024], P('panel', 'front'), may hold values from 0.6 to 1.2
Outputs:
- leaf_solution: float32 [16, 32, 32, 1024], P('panel', 'front')
- sep_solution: float32 [16, 32, 4096], P('panel', None, 'front')
The draws below stay inside these ranges and needn't reach their ends.
Inputs may be any that keep to these rules, and one draw needn't show every extreme that they name: `leaf_inverse`: each leaf inverse factor is dense; its diagonal entries lie near 0.8 to 1.1, and its off-diagonal part is not small in sum. `sep_inverse`: each separator inverse factor is dense; its diagonal entries lie near 0.8 to 1.1, and its off-diagonal part is not small in sum. `parent_map`: within one front the 512 entries are distinct; update rows o * 32 to (o + 1) * 32 - 1 of every front name only unknowns o * 256 to (o + 1) * 256 - 1; every separator unknown of a panel is named by exactly 4 fronts.
All inputs are finite; a program needn't handle non-finite values.
Results may differ from the reference program's by a relative error of at most 0.02.
Values may be sent and summed in bfloat16 or wider, within the bound.
A program may use at most 64 MiB of HBM per device.

```python
import math
import jax
import jax.numpy as jnp
from jax import lax

LEAF = 1024
UPD = 512
SEP = 4096
RHS = 32
FRONTS = 32
PANELS = 16
SHARE = 256
OWN_ROWS = 32


def with_diagonal(offdiag, diagonal):
    size = offdiag.shape[-1]
    ident = (jnp.arange(size)[:, None] == jnp.arange(size)[None, :]).astype(jnp.float32)
    return offdiag + ident * diagonal[..., None, :]


def draw_leaf_inverse(key, part):
    key = jax.random.fold_in(key, 5)
    first, second = jax.random.split(key)
    shape = (PANELS, FRONTS, LEAF, LEAF)
    diagonal = jax.random.uniform(first, (PANELS, FRONTS, LEAF), jnp.float32, 0.8, 1.1)
    offdiag = 0.5 * jax.random.normal(second, shape, jnp.float32) / math.sqrt(LEAF)
    return with_diagonal(offdiag, diagonal).astype(jnp.bfloat16)


def draw_sep_inverse(key, part):
    key = jax.random.fold_in(key, 7)
    first, second = jax.random.split(key)
    shape = (PANELS, SEP, SEP)
    diagonal = jax.random.uniform(first, (PANELS, SEP), jnp.float32, 0.8, 1.1)
    offdiag = 0.5 * jax.random.normal(second, shape, jnp.float32) / math.sqrt(SEP)
    return with_diagonal(offdiag, diagonal).astype(jnp.bfloat16)


def draw_parent_map(key, part):
    key = jax.random.fold_in(key, 11)
    owners = SEP // SHARE
    subkeys = jax.random.split(key, PANELS * owners)
    orders = jax.vmap(lambda single: jax.random.permutation(single, SHARE))(subkeys)
    orders = orders.reshape(PANELS, owners, SHARE)
    slot = (jnp.arange(FRONTS)[:, None] * OWN_ROWS + jnp.arange(OWN_ROWS)[None, :]) % SHARE
    chosen = orders[:, :, slot] + (jnp.arange(owners) * SHARE)[None, :, None, None]
    chosen = jnp.transpose(chosen, (0, 2, 1, 3)).reshape(PANELS, FRONTS, UPD)
    return chosen.astype(jnp.int32)


def level_of(stream_key, dims, pieces, low, top_value):
    def one(axis_at, parts):
        draws = jax.random.uniform(jax.random.fold_in(jax.random.fold_in(stream_key, 6), axis_at), (parts,), jnp.float32, low / len(pieces), top_value / len(pieces))
        return jnp.repeat(jnp.exp(draws), dims[axis_at] // parts).reshape((-1,) + (1,) * (len(dims) - axis_at - 1))

    factor_of = one(*pieces[0])
    for cut in pieces[1:]:
        factor_of = factor_of * one(*cut)
    return factor_of


def bell_draw(own_key, shape, spread, most, cuts=(), held_as=jnp.bfloat16):
    loudness = level_of(own_key, shape, cuts, -0.22, 0.18) if cuts else 1.0
    result = jax.random.normal(own_key, shape, jnp.float32) * spread * loudness
    return jnp.minimum(jnp.maximum(result, -most), most).astype(held_as)


def setup_inputs(seed: int = 0) -> dict:
    streams_of = jax.random.split(jax.random.key(seed), 10)
    source_leaf = bell_draw(streams_of[0], (PANELS, FRONTS, RHS, LEAF), 1.0, 6.0, ((0, 16), (1, 16)), jnp.float32)
    source_sep = bell_draw(streams_of[1], (PANELS, RHS, SEP), 1.0, 6.0, ((0, 16), (2, 16)), jnp.float32)
    leaf_inverse = draw_leaf_inverse(jax.random.fold_in(streams_of[9], 71), 0)
    lift = bell_draw(streams_of[3], (PANELS, FRONTS, LEAF, UPD), LEAF ** -0.5, 0.1875, ((0, 16), (1, 16)))
    lower = bell_draw(streams_of[4], (PANELS, FRONTS, UPD, LEAF), UPD ** -0.5, 0.25, ((0, 16), (1, 16)))
    sep_inverse = draw_sep_inverse(jax.random.fold_in(streams_of[9], 71), 0)
    parent_map = draw_parent_map(jax.random.fold_in(streams_of[9], 71), 0)
    couple_down = jnp.clip(0.6 + 0.6 * jax.random.uniform(streams_of[7], (PANELS, FRONTS, LEAF), jnp.float32) ** level_of(streams_of[7], (PANELS, FRONTS, LEAF), ((0, 16), (1, 16)), -0.2, 0.2), 0.6, 1.2)
    couple_up = jnp.clip(0.6 + 0.6 * jax.random.uniform(streams_of[8], (PANELS, FRONTS, LEAF), jnp.float32) ** level_of(streams_of[8], (PANELS, FRONTS, LEAF), ((0, 16), (1, 16)), -0.2, 0.2), 0.6, 1.2)
    return dict(source_leaf=source_leaf, source_sep=source_sep, leaf_inverse=leaf_inverse, lift=lift, lower=lower, sep_inverse=sep_inverse, parent_map=parent_map, couple_down=couple_down, couple_up=couple_up)


def leaf_apply(loaded, inverse):
    rounded = loaded.astype(jnp.bfloat16).astype(jnp.float32)
    return jnp.einsum("fbl,flm->fbm", rounded, inverse.astype(jnp.float32))


def reference(source_leaf, source_sep, leaf_inverse, lift, lower, sep_inverse, parent_map, couple_down, couple_up):
    zero_trace = jnp.zeros(source_leaf.shape[1:], jnp.bfloat16)

    def down_step(trace, inputs):
        source, inverse, coupling = inputs
        loaded = source + coupling[:, None, :] * trace.astype(jnp.float32)
        solved = leaf_apply(loaded, inverse)
        return solved.astype(jnp.bfloat16), loaded

    _, stored = lax.scan(down_step, zero_trace, (source_leaf, leaf_inverse, couple_down))

    def up_step(trace, inputs):
        loaded, inverse, coupling = inputs
        solved = leaf_apply(loaded + coupling[:, None, :] * trace.astype(jnp.float32), inverse)
        return solved.astype(jnp.bfloat16), solved

    _, swept = lax.scan(up_step, zero_trace, (stored, leaf_inverse, couple_up), reverse=True)

    def separate(inputs):
        solved, source, lifting, lowering, inverse, parents = inputs
        rounded = solved.astype(jnp.bfloat16).astype(jnp.float32)
        update = jnp.einsum("fbl,flu->fbu", rounded, lifting.astype(jnp.float32))
        flat = jnp.transpose(update, (1, 0, 2)).reshape(update.shape[1], -1)
        gathered = jnp.zeros((update.shape[1], SEP), jnp.float32).at[:, parents.reshape(-1)].add(flat)
        reduced = (source - gathered).astype(jnp.bfloat16)
        sep_solved = jnp.dot(reduced, inverse, preferred_element_type=jnp.float32)
        picked = sep_solved.astype(jnp.bfloat16)[:, parents].astype(jnp.float32)
        back = jnp.einsum("bfu,ful->fbl", picked, lowering.astype(jnp.float32))
        return solved - back, sep_solved

    leaf_solution, sep_solution = lax.map(separate, (swept, source_sep, lift, lower, sep_inverse, parent_map))
    return leaf_solution, sep_solution
```

```python
import jax
import jax.numpy as jnp
from jax import lax
from jax.experimental import pallas as pl
from jax.experimental.pallas import tpu as pltpu
from jax.sharding import PartitionSpec as P

MESH = pl.DeviceIdType.MESH
F32 = jnp.float32
BF16 = jnp.bfloat16
LEAF = 1024
UPD = 512
SHARE = 256
RHS = 32
ROWS = 32
PEERS = 16
LAST = 7
DIRECT = 3
HALF = 16
WAVES = 4
CHUNK = 256
CHUNKS = LEAF // CHUNK

S_CP, S_SRC, S_A, S_PM, S_SS, S_LIFT, S_SEP, S_P, S_Q, S_UA, S_OUT = 0, 1, 2, 4, 5, 6, 7, 8, 10, 12, 13


def dot(a, b):
    return jnp.dot(a, b, preferred_element_type=F32)


def dot_t(a, b):
    return lax.dot_general(a, b, (((1,), (1,)), ((), ())), preferred_element_type=F32)


def kernel(
    src, ssep, inv, lift, lower, sepinv, pm, cd, cu,
    leaf_out, sep_out,
    A, PP, QQ, LL, LW, SS, SL, CP, CT, PM, SRC_S,
    T, U, TS, US, E, DB, G, UA, UB,
    Z, PMS, PMR, UPS, UPR, ONE, RED, PKS, PKR, SEPA,
    lsem, ps, pr, dsnd, drcv, usnd, urcv, asnd, arcv,
):
    p = lax.axis_index("panel")
    me = lax.axis_index("front")
    core = lax.rem(p, 2)
    c = p // 2
    pair = (p + 1 - 2 * core, me)
    is0 = core == 0
    is1 = core == 1
    first = c == 0
    last = c == LAST

    def remote(s, d, ss, rs, dev):
        return pltpu.make_async_remote_copy(
            src_ref=s, dst_ref=d, send_sem=ss, recv_sem=rs, device_id=dev, device_id_type=MESH
        )

    def to_pair(s, d, i):
        return remote(s, d, ps.at[i], pr.at[i], pair)

    own = [pltpu.make_async_copy(inv.at[f], A.at[core, f], lsem.at[f]) for f in range(2)]
    own_lift = pltpu.make_async_copy(lift, LL.at[1], lsem.at[2])
    own_lower = pltpu.make_async_copy(lower, LW, lsem.at[3])
    own_sep = pltpu.make_async_copy(sepinv, SS.at[1], lsem.at[4])
    for copy in own:
        copy.start()

    barrier = pltpu.get_barrier_semaphore()

    def greet(k, _):
        pl.semaphore_signal(
            barrier, inc=1, device_id=(2 * c + 1, lax.rem(me + k, PEERS)), device_id_type=MESH
        )
        return 0

    @pl.when(is0)
    def _():
        greet(0, 0)

    @pl.when(is1)
    def _():
        pl.semaphore_signal(barrier, inc=1, device_id=pair, device_id_type=MESH)

        @pl.when(c > 0)
        def _():
            pl.semaphore_signal(barrier, inc=1, device_id=(p - 2, me), device_id_type=MESH)

        @pl.when(c < LAST)
        def _():
            pl.semaphore_signal(barrier, inc=1, device_id=(p + 2, me), device_id_type=MESH)

    lax.fori_loop(1, PEERS, greet, 0)
    CP[core, 0:2, :] = cd[...]
    CP[core, 2:4, :] = cu[...]
    PM[core, 0:2, :] = pm[...].astype(F32)
    ends = jnp.where(first, 0, 1) + jnp.where(last, 0, 1)
    pl.semaphore_wait(barrier, jnp.where(is1, 2 * PEERS - 1 + ends, 1))

    send_a = [to_pair(inv.at[f], A.at[core, f], S_A + f) for f in range(2)]
    got_a = [to_pair(inv.at[f], A.at[1 - core, f], S_A + f) for f in range(2)]
    send_cp = to_pair(CP.at[core], CP.at[core], S_CP)
    got_cp = to_pair(CP.at[core], CP.at[1 - core], S_CP)
    send_src = to_pair(src, SL, S_SRC)
    send_pm = to_pair(PM.at[0], PM.at[0], S_PM)
    send_ss = to_pair(ssep, SRC_S, S_SS)
    send_lift = to_pair(lift, LL.at[0], S_LIFT)
    send_sep = to_pair(sepinv, SS.at[0], S_SEP)
    ship_p = [to_pair(PP.at[f], PP.at[f], S_P + f) for f in range(2)]
    ship_q = [to_pair(QQ.at[f], QQ.at[f], S_Q + f) for f in range(2)]
    ship_ua = to_pair(UA, UA, S_UA)
    ship_out = to_pair(SEPA, SEPA, S_OUT)

    send_cp.start()

    def finish(x, sweep):
        pt = PKR[...].astype(F32).reshape(UPD, 128).T.astype(BF16)
        for f in range(2):
            r = (2 * x + f) * RHS
            leaf_out[f] = sweep[f] - dot(pt[r : r + RHS, :], LW[f])

    @pl.when(is0)
    def _core0():
        send_src.start()
        send_a[0].start()
        send_a[1].start()
        send_pm.start()
        send_ss.start()
        own_lower.start()
        got_cp.wait_recv()
        for x in range(2):
            CT[x] = CP[x].T
        for f in range(2):
            own[f].wait()
            got_a[f].wait_recv()

            @pl.loop(0, 4)
            def _(b):
                rows = pl.ds(pl.multiple_of(b * 256, 256), 256)
                left = (A[0, f, rows, :].astype(F32) * CP[1, f : f + 1, :]).astype(BF16)
                PP[f, rows, :] = (dot(left, A[1, f]) * CT[0, rows, f : f + 1]).astype(BF16)
                to_pair(PP.at[f, rows], PP.at[f, rows], S_P + f).start()

        send_lift.start()
        send_sep.start()
        for f in range(2):

            @pl.loop(0, 4)
            def _(b):
                rows = pl.ds(pl.multiple_of(b * 256, 256), 256)
                base = jnp.where(last, PP[f, rows, :].astype(F32), A[1, f, rows, :].astype(F32))
                left = (base * CP[0, f + 2 : f + 3, :]).astype(BF16)
                scale = jnp.where(last, 1.0, CT[1, rows, f + 2 : f + 3])
                extra = jnp.where(last, CT[0, rows, f : f + 1], 0.0)
                full = dot(left, A[0, f]) * scale + extra * A[0, f, rows, :].astype(F32)
                QQ[f, rows, :] = full.astype(BF16)
                to_pair(QQ.at[f, rows], QQ.at[f, rows], S_Q + f).start()

        for copy in (send_cp, send_src, *send_a, send_pm, send_ss, send_lift, send_sep, *ship_p, *ship_q):
            copy.wait_send()
        own_lower.wait()
        ship_ua.wait_recv()
        ship_out.wait_recv()
        sep_out[...] = SEPA[...]
        remote(PKR, PKR, asnd.at[3], arcv.at[3], pair).wait_recv()
        finish(0, UA)

    def wave_of(w):
        return w // 2, pl.ds(pl.multiple_of(lax.rem(w, 2) * HALF, HALF), HALF)

    @pl.when(is1)
    def _core1():
        send_a[0].start()
        send_a[1].start()
        own_lift.start()
        own_sep.start()
        own_lower.start()

        below = (p + 2, me)
        above = (p - 2, me)

        def down_wave(w, cols=slice(None)):
            f, rows = wave_of(w)
            return remote(TS.at[f, rows, cols], T.at[f, rows, cols], dsnd.at[w], drcv.at[w], below)

        def up_wave(w, cols=slice(None)):
            f, rows = wave_of(w)
            return remote(US.at[f, rows, cols], U.at[f, rows, cols], usnd.at[w], urcv.at[w], above)

        def coupled(x, f, k):
            return CP[x, pl.ds(f + k, 1), :]

        got_cp.wait_recv()
        send_pm.wait_recv()
        Z[...] = jnp.zeros_like(Z)
        Z[0:2, :] = PM[0, 0:2, :]
        Z[2:4, :] = PM[1, 0:2, :]
        PMS[...] = Z[...].T

        def exchange(k, out, into, lane, target_core):
            o = lax.rem(me + k, PEERS)
            rows = pl.ds(pl.multiple_of(o * ROWS, ROWS), ROWS)
            return remote(
                out.at[rows], into.at[me], asnd.at[lane], arcv.at[lane], (2 * c + target_core, o)
            )

        def all_to_all(out, into, lane):
            def one(k, _):
                exchange(k, out, into, lane, 1).start()
                return 0

            lax.fori_loop(1, PEERS, one, 0)
            into[me] = out[pl.ds(pl.multiple_of(me * ROWS, ROWS), ROWS), :]

        def arrived(into, lane):
            part = into.at[pl.ds(0, PEERS - 1)]
            return remote(part, part, asnd.at[lane], arcv.at[lane], pair)

        all_to_all(PMS, PMR, 0)

        def build_maps():
            arrived(PMR, 0).wait()
            table = PMR[...].reshape(UPD, 128)
            column = (lax.broadcasted_iota(jnp.int32, (UPD, SHARE), 1) + me * SHARE).astype(F32)
            for q in range(4):
                ONE[q] = jnp.where(table[:, q : q + 1] == column, 1.0, 0.0).astype(BF16)

        send_src.wait_recv()
        for f in range(2):
            got_a[f].wait_recv()
            own[f].wait()

        @pl.when(first)
        def _():
            T[...] = jnp.zeros_like(T)

        @pl.when(c <= DIRECT)
        def _():
            def step(w, _):
                f, rows = wave_of(w)

                @pl.when(c > 0)
                def _():
                    down_wave(w).wait_recv()

                loaded = SL[f, rows, :] + coupled(0, f, 0) * T[f, rows, :].astype(F32)
                middle = dot(loaded.astype(BF16), A[0, f])
                loaded = src[f, rows, :] + coupled(1, f, 0) * middle.astype(BF16).astype(F32)
                loaded = loaded.astype(BF16)
                for j in range(CHUNKS):
                    cols = slice(j * CHUNK, (j + 1) * CHUNK)
                    out = dot(loaded, A[1, f, :, cols])
                    DB[f, rows, cols] = out
                    TS[f, rows, cols] = out.astype(BF16)
                    down_wave(w, cols).start()
                return 0

            lax.fori_loop(0, WAVES, step, 0)
            build_maps()

        @pl.when(c > DIRECT)
        def _():
            def alone(f, _):
                middle = dot(SL[f].astype(BF16), A[0, f])
                loaded = src[f] + coupled(1, f, 0) * middle.astype(BF16).astype(F32)
                out = dot(loaded.astype(BF16), A[1, f])
                DB[f] = out
                E[f] = out

                @pl.when(last)
                def _():
                    loaded = SL[f] + coupled(0, f, 2) * out.astype(BF16).astype(F32)
                    E[f] = dot(loaded.astype(BF16), A[0, f])

                return 0

            lax.fori_loop(0, 2, alone, 0)
            build_maps()

            def sweep(weight, keep, half, copy_of):
                def step(w, _):
                    f, rows = wave_of(w)
                    down_wave(w).wait_recv()
                    t = T[f, rows, :]
                    for j in range(CHUNKS):
                        cols = slice(j * CHUNK, (j + 1) * CHUNK)
                        out = dot(t, weight[f, :, cols]) + E[f, rows, cols]
                        keep[f, rows, cols] = out
                        half[f, rows, cols] = out.astype(BF16)
                        copy_of(w, cols).start()
                    return 0

                lax.fori_loop(0, WAVES, step, 0)

            for f in range(2):
                ship_p[f].wait_recv()

            @pl.when(c < LAST)
            def _():
                sweep(PP, DB, TS, down_wave)

            @pl.when(last)
            def _():
                for f in range(2):
                    ship_q[f].wait_recv()
                sweep(QQ, UA, US, up_wave)

                def rest(f, _):
                    UB[f] = DB[f] + dot(T[f], PP[f])
                    return 0

                lax.fori_loop(0, 2, rest, 0)

        @pl.when(c <= DIRECT)
        def _():
            for f in range(2):
                ship_p[f].wait_recv()

        @pl.when(c < LAST)
        def _():
            def before(f, _):
                loaded = (
                    SL[f]
                    + coupled(0, f, 0) * T[f].astype(F32)
                    + coupled(0, f, 2) * DB[f].astype(BF16).astype(F32)
                )
                G[f] = dot(loaded.astype(BF16), A[0, f])
                return 0

            lax.fori_loop(0, 2, before, 0)
            for f in range(2):
                ship_q[f].wait_recv()

            def step(w, _):
                f, rows = wave_of(w)
                up_wave(w).wait_recv()
                t = U[f, rows, :]
                for j in range(CHUNKS):
                    cols = slice(j * CHUNK, (j + 1) * CHUNK)
                    out = dot(t, QQ[f, :, cols]) + G[f, rows, cols]
                    UA[f, rows, cols] = out
                    US[f, rows, cols] = out.astype(BF16)

                    @pl.when(c > 0)
                    def _():
                        up_wave(w, cols).start()

                return 0

            lax.fori_loop(0, WAVES, step, 0)

            def rest(f, _):
                loaded = coupled(1, f, 2) * U[f].astype(F32)
                UB[f] = DB[f] + dot(loaded.astype(BF16), A[1, f])
                return 0

            lax.fori_loop(0, 2, rest, 0)

        ship_ua.start()
        send_lift.wait_recv()
        own_lift.wait()
        for x, swept in enumerate((UA, UB)):
            for f in range(2):
                r = (2 * x + f) * RHS
                Z[r : r + RHS, :] = dot(swept[f].astype(BF16), LL[x, f])
        UPS[...] = Z[...].T.astype(BF16)
        all_to_all(UPS, UPR, 1)
        send_ss.wait_recv()
        arrived(UPR, 1).wait()
        updates = UPR[...].astype(F32).reshape(UPD, 128).T.astype(BF16)
        for x, source in enumerate((SRC_S, ssep)):
            r = 2 * x * RHS
            gathered = dot(updates[r : r + RHS, :], ONE[2 * x])
            gathered += dot(updates[r + RHS : r + 2 * RHS, :], ONE[2 * x + 1])
            RED[me, x * RHS : (x + 1) * RHS, :] = (source[...] - gathered).astype(BF16)

        def spread(k, _):
            o = lax.rem(me + k, PEERS)
            remote(RED.at[me], RED.at[me], asnd.at[2], arcv.at[2], (p, o)).start()
            return 0

        lax.fori_loop(1, PEERS, spread, 0)
        send_sep.wait_recv()
        own_sep.wait()
        arrived(RED, 2).wait()
        for x in range(2):
            total = jnp.zeros((RHS, SHARE), F32)
            for s in range(PEERS):
                total += dot(
                    RED[s, x * RHS : (x + 1) * RHS, :], SS[x, s * SHARE : (s + 1) * SHARE, :]
                )
            if x == 0:
                SEPA[...] = total
            else:
                sep_out[...] = total
            half = total.astype(BF16)
            for f in range(2):
                r = (2 * x + f) * RHS
                Z[r : r + RHS, :] = dot_t(half, ONE[2 * x + f])
        PKS[...] = Z[...].T.astype(BF16)
        ship_out.start()

        def pick(k, _):
            exchange(k, PKS, PKR, 3, 0).start()
            return 0

        lax.fori_loop(0, PEERS, pick, 0)
        all_to_all(PKS, PKR, 4)
        own_lower.wait()
        arrived(PKR, 4).wait()
        finish(1, UB)

        for copy in (send_cp, *send_a, ship_ua, ship_out):
            copy.wait_send()
        remote(PKR, PKR, asnd.at[3], arcv.at[3], pair).wait_send()

        def sent_down(w, _):
            down_wave(w).wait_send()
            return 0

        def sent_up(w, _):
            up_wave(w).wait_send()
            return 0

        @pl.when(c < LAST)
        def _():
            lax.fori_loop(0, WAVES, sent_down, 0)

        @pl.when(c > 0)
        def _():
            lax.fori_loop(0, WAVES, sent_up, 0)


def local(source_leaf, source_sep, leaf_inverse, lift, lower, sep_inverse, parent_map, couple_down, couple_up):
    vmem = pl.BlockSpec(memory_space=pltpu.VMEM)
    hbm = pl.BlockSpec(memory_space=pl.ANY)
    trace = (2, RHS, LEAF)
    leaf, sep = pl.pallas_call(
        kernel,
        out_shape=(
            jax.ShapeDtypeStruct(trace, F32),
            jax.ShapeDtypeStruct((RHS, SHARE), F32),
        ),
        in_specs=[vmem, vmem, hbm, hbm, hbm, hbm, vmem, vmem, vmem],
        out_specs=(vmem, vmem),
        scratch_shapes=[
            pltpu.VMEM((2, 2, LEAF, LEAF), BF16),
            pltpu.VMEM((2, LEAF, LEAF), BF16),
            pltpu.VMEM((2, LEAF, LEAF), BF16),
            pltpu.VMEM((2, 2, LEAF, UPD), BF16),
            pltpu.VMEM((2, UPD, LEAF), BF16),
            pltpu.VMEM((2, PEERS * SHARE, SHARE), BF16),
            pltpu.VMEM(trace, F32),
            pltpu.VMEM((2, 8, LEAF), F32),
            pltpu.VMEM((2, LEAF, 8), F32),
            pltpu.VMEM((2, 8, UPD), F32),
            pltpu.VMEM((RHS, SHARE), F32),
            *[pltpu.VMEM(trace, BF16) for _ in range(4)],
            *[pltpu.VMEM(trace, F32) for _ in range(5)],
            pltpu.VMEM((128, UPD), F32),
            pltpu.VMEM((UPD, 128), F32),
            pltpu.VMEM((PEERS, ROWS, 128), F32),
            pltpu.VMEM((UPD, 128), BF16),
            pltpu.VMEM((PEERS, ROWS, 128), BF16),
            pltpu.VMEM((4, UPD, SHARE), BF16),
            pltpu.VMEM((PEERS, 2 * RHS, SHARE), BF16),
            pltpu.VMEM((UPD, 128), BF16),
            pltpu.VMEM((PEERS, ROWS, 128), BF16),
            pltpu.VMEM((RHS, SHARE), F32),
            pltpu.SemaphoreType.DMA((5,)),
            pltpu.SemaphoreType.DMA((14,)),
            pltpu.SemaphoreType.DMA((14,)),
            pltpu.SemaphoreType.DMA((WAVES,)),
            pltpu.SemaphoreType.DMA((WAVES,)),
            pltpu.SemaphoreType.DMA((WAVES,)),
            pltpu.SemaphoreType.DMA((WAVES,)),
            pltpu.SemaphoreType.DMA((5,)),
            pltpu.SemaphoreType.DMA((5,)),
        ],
        compiler_params=pltpu.CompilerParams(
            collective_id=0, has_side_effects=True, vmem_limit_bytes=56 * 1024 * 1024
        ),
        name="sweep",
    )(
        source_leaf[0], source_sep[0], leaf_inverse[0], lift[0], lower[0],
        sep_inverse[0], parent_map[0], couple_down[0], couple_up[0],
    )
    return leaf[None], sep[None]


def solution(mesh):
    return jax.shard_map(
        local,
        mesh=mesh,
        in_specs=(
            P("panel", "front", None, None),
            P("panel", None, "front"),
            P("panel", "front", None, None),
            P("panel", "front", None, None),
            P("panel", "front", None, None),
            P("panel", None, "front"),
            P("panel", "front", None),
            P("panel", "front", None),
            P("panel", "front", None),
        ),
        out_specs=(P("panel", "front", None, None), P("panel", None, "front")),
        check_vma=False,
    )
```

```python
import functools

import jax
import jax.numpy as jnp
from jax import lax
from jax.experimental import pallas as pl
from jax.experimental.pallas import tpu as pltpu
from jax.sharding import PartitionSpec as P

MESH = pl.DeviceIdType.MESH
F32 = jnp.float32
BF16 = jnp.bfloat16
LEAF = 1024
UPD = 512
SHARE = 256
RHS = 32
ROWS = 16
GROUP = 4
PEERS = 16
LAST = 7
DIRECT = 3
HALF = 16
WAVES = 4
CHUNK = 512
CHUNKS = LEAF // CHUNK

S_CP, S_SRC, S_A, S_LIFT, S_P, S_Q, S_UA, S_DA = 0, 1, 2, 4, 5, 7, 9, 10


def dot(a, b):
    return jnp.dot(a, b, preferred_element_type=F32)


def dot_t(a, b):
    return lax.dot_general(a, b, (((1,), (1,)), ((), ())), preferred_element_type=F32)


def kernel(
    src, ssep, inv, lift, lower, sepinv, pm, cd, cu,
    leaf_out, sep_out,
    A, PP, QQ, LL, LW, SS, SL, CP, CT,
    T, U, TS, US, DA, E, DB, G, UA, UB,
    Z, ZP, PMS, PMR, UPS, UPR, ONE, RED, PKS, PKR,
    lsem, ps, pr, dsnd, drcv, usnd, urcv, osnd, orcv, rsnd, rrcv,
):
    p = lax.axis_index("panel")
    me = lax.axis_index("front")
    core = lax.rem(p, 2)
    c = p // 2
    pair = (p + 1 - 2 * core, me)
    is0 = core == 0
    is1 = core == 1
    first = c == 0
    last = c == LAST
    def remote(s, d, ss, rs, dev):
        return pltpu.make_async_remote_copy(
            src_ref=s, dst_ref=d, send_sem=ss, recv_sem=rs, device_id=dev, device_id_type=MESH
        )

    def to_pair(s, d, i):
        return remote(s, d, ps.at[i], pr.at[i], pair)

    own = [pltpu.make_async_copy(inv.at[f], A.at[core, f], lsem.at[f]) for f in range(2)]
    own_lift = pltpu.make_async_copy(lift, LL.at[1], lsem.at[2])
    own_lower = [
        pltpu.make_async_copy(lower.at[f, :, h], LW.at[f, h], lsem.at[4 + 2 * f + h])
        for f in range(2)
        for h in range(2)
    ]
    own_sep = pltpu.make_async_copy(sepinv, SS, lsem.at[3])
    for copy in own:
        copy.start()

    barrier = pltpu.get_barrier_semaphore()

    def signal(dev):
        pl.semaphore_signal(barrier, inc=1, device_id=dev, device_id_type=MESH)

    @pl.when(is1)
    def _():
        @pl.when(c < LAST)
        def _():
            signal((p + 2, me))

        @pl.when(c > 0)
        def _():
            signal((p - 2, me))

        signal(pair)

    def greet(k, _):
        o = lax.rem(me + k, PEERS)

        @pl.when(k > 0)
        def _():
            signal((p, o))

        @pl.when(is0)
        def _():
            signal((p + 1, o))

        return 0

    lax.fori_loop(0, PEERS, greet, 0)
    CP[core, 0:2, :] = cd[...]
    CP[core, 2:4, :] = cu[...]
    Z[...] = jnp.zeros_like(Z)
    Z[0:2, :] = pm[...].astype(F32)
    Z[2:4, :] = pm[...].astype(F32)
    targets = Z[...].T.reshape(PEERS, 2, ROWS, 128)
    lane = lax.broadcasted_iota(jnp.int32, (PEERS, ROWS, 128), 2)
    PMS[...] = jnp.where(lane < 2, targets[:, 0], targets[:, 1]).reshape(PEERS * ROWS, 128)

    @pl.when(jnp.logical_and(is0, first))
    def _():
        for f in range(2):
            own[f].wait()
            DA[f] = dot(src[f].astype(BF16), A[0, f]).astype(BF16)

    ends = jnp.where(first, 0, 1) + jnp.where(last, 0, 1)
    far = PEERS + ends
    pl.semaphore_wait(barrier, PEERS - 1 + jnp.where(is1, far, 1))

    send_a = [to_pair(inv.at[f], A.at[core, f], S_A + f) for f in range(2)]
    got_a = [to_pair(inv.at[f], A.at[1 - core, f], S_A + f) for f in range(2)]
    send_cp = to_pair(CP.at[core], CP.at[core], S_CP)
    got_cp = to_pair(CP.at[core], CP.at[1 - core], S_CP)
    send_src = to_pair(src, SL, S_SRC)
    send_lift = to_pair(lift, LL.at[0], S_LIFT)
    ship_p = [to_pair(PP.at[f], PP.at[f], S_P + f) for f in range(2)]
    ship_q = [to_pair(QQ.at[f], QQ.at[f], S_Q + f) for f in range(2)]
    ship_ua = to_pair(UA, UA, S_UA)
    ship_da = [to_pair(DA.at[f], DA.at[f], S_DA + f) for f in range(2)]
    def part(k):
        return pl.ds(pl.multiple_of(k * ROWS, ROWS), ROWS)

    def to_owners(out, into, lane, target, to_self):
        def one(k, _):
            o = lax.rem(me + k, PEERS)
            remote(
                out.at[part(o)], into.at[me], osnd.at[lane], orcv.at[lane], (2 * c + target, o)
            ).start()
            return 0

        lax.fori_loop(0 if to_self else 1, PEERS, one, 0)
        if not to_self:
            into[me] = out[part(me), :]

    def several(ref, n, lane):
        some = ref.at[pl.ds(0, n)]
        return remote(some, some, osnd.at[lane], orcv.at[lane], pair)

    def send_targets():
        to_owners(PMS, PMR, 3, core, False)

    def build_maps():
        several(PMR, PEERS - 1, 3).wait()
        table = PMR[...].reshape(SHARE, 128)
        column = (lax.broadcasted_iota(jnp.int32, (SHARE, SHARE), 1) + me * SHARE).astype(F32)
        for q in range(4):
            ONE[q] = jnp.where(table[:, q : q + 1] == column, 1.0, 0.0).astype(BF16)

    def turned(ref):
        return ref[...].astype(F32).reshape(SHARE, 128).T.astype(BF16)

    def separator(x, swept):
        several(UPR, PEERS - x, 4 + x).wait_recv()
        updates = turned(UPR)
        gathered = jnp.zeros((RHS, SHARE), F32)
        for q in range(4):
            gathered += dot(updates[q * RHS : (q + 1) * RHS, :], ONE[q])
        RED[me] = (ssep[...] - gathered).astype(BF16)

        def spread(k):
            o = lax.rem(me + k, PEERS)
            return remote(RED.at[me], RED.at[me], rsnd.at[k], rrcv.at[k], (p, o))

        for k in range(1, PEERS):
            spread(k).start()
        own_sep.wait()
        total = jnp.zeros((RHS, SHARE), F32)
        for group in range(0, PEERS, GROUP):
            sources = [lax.rem(me + PEERS - k, PEERS) for k in range(group, group + GROUP)]
            for k, w in zip(range(group, group + GROUP), sources):
                if k:
                    remote(RED.at[w], RED.at[w], rsnd.at[k], rrcv.at[k], pair).wait_recv()
            for w in sources:
                total += dot(RED[w], SS[pl.ds(pl.multiple_of(w * SHARE, SHARE), SHARE), :])
        half = total.astype(BF16)
        for q in range(4):
            ZP[q * RHS : (q + 1) * RHS, :] = dot_t(half, ONE[q])
        PKS[...] = ZP[...].T.astype(BF16)
        to_owners(PKS, PKR, 6, x, False)
        sep_out[...] = total
        for copy in own_lower:
            copy.wait()
        if x == 0:
            ship_ua.wait_recv()
        several(PKR, PEERS - 1, 6).wait()
        picked = turned(PKR)
        for f in range(2):
            back = dot(picked[f * RHS : (f + 1) * RHS, :], LW[f, 0].reshape(SHARE, LEAF))
            back += dot(picked[(2 + f) * RHS : (3 + f) * RHS, :], LW[f, 1].reshape(SHARE, LEAF))
            leaf_out[f] = swept[f] - back
        for k in range(1, PEERS):
            spread(k).wait_send()

    @pl.when(is0)
    def _core0():
        @pl.when(first)
        def _():
            for copy in ship_da:
                copy.start()

        send_cp.start()
        send_src.start()
        send_a[0].start()
        send_a[1].start()
        send_targets()
        own_sep.start()
        for copy in own_lower:
            copy.start()
        got_cp.wait_recv()
        for x in range(2):
            CT[x] = CP[x].T
        for f in range(2):

            @pl.when(c > 0)
            def _():
                own[f].wait()

            got_a[f].wait_recv()

        @pl.when(c > DIRECT)
        def _():
            for f in range(2):

                @pl.loop(0, 4)
                def _(b):
                    rows = pl.ds(pl.multiple_of(b * 256, 256), 256)
                    left = (A[0, f, rows, :].astype(F32) * CP[1, f : f + 1, :]).astype(BF16)
                    PP[f, rows, :] = (dot(left, A[1, f]) * CT[0, rows, f : f + 1]).astype(BF16)
                    to_pair(PP.at[f, rows], PP.at[f, rows], S_P + f).start()

        send_lift.start()
        for f in range(2):

            @pl.loop(0, 4)
            def _(b):
                rows = pl.ds(pl.multiple_of(b * 256, 256), 256)
                base = jnp.where(last, PP[f, rows, :].astype(F32), A[1, f, rows, :].astype(F32))
                left = (base * CP[0, f + 2 : f + 3, :]).astype(BF16)
                scale = jnp.where(last, 1.0, CT[1, rows, f + 2 : f + 3])
                extra = jnp.where(last, CT[0, rows, f : f + 1], 0.0)
                full = dot(left, A[0, f]) * scale + extra * A[0, f, rows, :].astype(F32)
                QQ[f, rows, :] = full.astype(BF16)
                to_pair(QQ.at[f, rows], QQ.at[f, rows], S_Q + f).start()

        build_maps()
        separator(0, UA)
        for copy in (send_cp, send_src, *send_a, send_lift, *ship_q):
            copy.wait_send()

        @pl.when(c > DIRECT)
        def _():
            for copy in ship_p:
                copy.wait_send()

        @pl.when(first)
        def _():
            for copy in ship_da:
                copy.wait_send()

    def wave_of(w):
        return w // 2, slice(w % 2 * HALF, w % 2 * HALF + HALF)

    @pl.when(is1)
    def _core1():
        send_cp.start()
        send_a[0].start()
        send_a[1].start()
        send_targets()
        own_sep.start()
        own_lift.start()
        for copy in own_lower:
            copy.start()

        below = (p + 2, me)
        above = (p - 2, me)

        def down_wave(w, cols=slice(None)):
            f, rows = wave_of(w)
            return remote(TS.at[f, rows, cols], T.at[f, rows, cols], dsnd.at[w], drcv.at[w], below)

        def up_wave(w, cols=slice(None)):
            f, rows = wave_of(w)
            return remote(US.at[f, rows, cols], U.at[f, rows, cols], usnd.at[w], urcv.at[w], above)

        def coupled(x, f, k):
            return CP[x, pl.ds(f + k, 1), :]

        def each_wave(step):
            for w in range(WAVES):
                step(w)

        def solve(w, left, weight, extra, keep, half, copy_of):
            f, rows = wave_of(w)
            parts = [slice(j * CHUNK, (j + 1) * CHUNK) for j in range(CHUNKS)]
            outs = []
            for cols in parts:
                out = dot(left, weight[f, :, cols])
                outs.append(out if extra is None else out + extra[f, rows, cols])
            for cols, out in zip(parts, outs):
                half[f, rows, cols] = out.astype(BF16)
                if copy_of is not None:
                    copy_of(w, cols).start()
            for cols, out in zip(parts, outs):
                keep[f, rows, cols] = out

        got_cp.wait_recv()

        @pl.when(first)
        def _():
            T[...] = jnp.zeros_like(T)

            def step(w):
                f, rows = wave_of(w)
                if w % 2 == 0:
                    own[f].wait()
                    ship_da[f].wait_recv()
                loaded = src[f, rows, :] + coupled(1, f, 0) * DA[f, rows, :].astype(F32)
                solve(w, loaded.astype(BF16), A.at[1], None, DB, TS, down_wave)

            each_wave(step)
            send_src.wait_recv()
            for f in range(2):
                got_a[f].wait_recv()

        @pl.when(jnp.logical_and(c > 0, c <= DIRECT))
        def _():
            send_src.wait_recv()

            def step(w):
                f, rows = wave_of(w)
                if w % 2 == 0:
                    got_a[f].wait_recv()
                    own[f].wait()
                down_wave(w).wait_recv()
                loaded = SL[f, rows, :] + coupled(0, f, 0) * T[f, rows, :].astype(F32)
                middle = dot(loaded.astype(BF16), A[0, f])
                loaded = src[f, rows, :] + coupled(1, f, 0) * middle.astype(BF16).astype(F32)
                solve(w, loaded.astype(BF16), A.at[1], None, DB, TS, down_wave)

            each_wave(step)

        @pl.when(c <= DIRECT)
        def _():
            build_maps()

        @pl.when(c > DIRECT)
        def _():
            send_src.wait_recv()
            for f in range(2):
                got_a[f].wait_recv()
                own[f].wait()

            def alone(f, _):
                middle = dot(SL[f].astype(BF16), A[0, f])
                loaded = src[f] + coupled(1, f, 0) * middle.astype(BF16).astype(F32)
                out = dot(loaded.astype(BF16), A[1, f])
                DB[f] = out
                E[f] = out

                @pl.when(last)
                def _():
                    loaded = SL[f] + coupled(0, f, 2) * out.astype(BF16).astype(F32)
                    E[f] = dot(loaded.astype(BF16), A[0, f])

                return 0

            lax.fori_loop(0, 2, alone, 0)
            build_maps()

            def sweep(weight, keep, half, copy_of):
                def step(w):
                    f, rows = wave_of(w)
                    down_wave(w).wait_recv()
                    solve(w, T[f, rows, :], weight, E, keep, half, copy_of)

                each_wave(step)

            for f in range(2):
                ship_p[f].wait_recv()

            @pl.when(c < LAST)
            def _():
                sweep(PP, DB, TS, down_wave)

            @pl.when(last)
            def _():
                for f in range(2):
                    ship_q[f].wait_recv()
                sweep(QQ, UA, US, up_wave)

        @pl.when(c < LAST)
        def _():
            def before(f, _):
                loaded = (
                    SL[f]
                    + coupled(0, f, 0) * T[f].astype(F32)
                    + coupled(0, f, 2) * DB[f].astype(BF16).astype(F32)
                )
                G[f] = dot(loaded.astype(BF16), A[0, f])
                return 0

            lax.fori_loop(0, 2, before, 0)
            for f in range(2):
                ship_q[f].wait_recv()

            def step(copy_of, w):
                f, rows = wave_of(w)
                up_wave(w).wait_recv()
                solve(w, U[f, rows, :], QQ, G, UA, US, copy_of)

            @pl.when(first)
            def _():
                each_wave(functools.partial(step, None))

            @pl.when(c > 0)
            def _():
                each_wave(functools.partial(step, up_wave))

        def lifted(x, half):
            for f in range(2):
                Z[f * RHS : (f + 1) * RHS, :] = dot(half[f], LL[x, f])
            rows = Z[0 : 2 * RHS, :].T.reshape(PEERS, 2, ROWS, 2 * RHS)
            packed = jnp.concatenate([rows[:, 0], rows[:, 1]], axis=-1)
            UPS[x] = packed.reshape(SHARE, 128).astype(BF16)
            to_owners(UPS.at[x], UPR, 4 + x, x, x == 0)

        send_lift.wait_recv()
        own_lift.wait()
        lifted(0, US)
        ship_ua.start()

        @pl.when(last)
        def _():
            def rest(f, _):
                UB[f] = DB[f] + dot(T[f], PP[f])
                return 0

            lax.fori_loop(0, 2, rest, 0)

        @pl.when(c < LAST)
        def _():
            def rest(f, _):
                loaded = coupled(1, f, 2) * U[f].astype(F32)
                UB[f] = DB[f] + dot(loaded.astype(BF16), A[1, f])
                return 0

            lax.fori_loop(0, 2, rest, 0)

        for f in range(2):
            DA[f] = UB[f].astype(BF16)
        lifted(1, DA)
        separator(1, UB)

        for copy in (send_cp, *send_a, ship_ua):
            copy.wait_send()
        several(UPR, PEERS, 4).wait_send()
        several(UPR, PEERS - 1, 5).wait_send()

        @pl.when(c < LAST)
        def _():
            each_wave(lambda w: down_wave(w).wait_send())

        @pl.when(c > 0)
        def _():
            each_wave(lambda w: up_wave(w).wait_send())


def local(source_leaf, source_sep, leaf_inverse, lift, lower, sep_inverse, parent_map, couple_down, couple_up):
    vmem = pl.BlockSpec(memory_space=pltpu.VMEM)
    hbm = pl.BlockSpec(memory_space=pl.ANY)
    trace = (2, RHS, LEAF)
    leaf, sep = pl.pallas_call(
        kernel,
        out_shape=(
            jax.ShapeDtypeStruct(trace, F32),
            jax.ShapeDtypeStruct((RHS, SHARE), F32),
        ),
        in_specs=[vmem, vmem, hbm, hbm, hbm, hbm, vmem, vmem, vmem],
        out_specs=(vmem, vmem),
        scratch_shapes=[
            pltpu.VMEM((2, 2, LEAF, LEAF), BF16),
            pltpu.VMEM((2, LEAF, LEAF), BF16),
            pltpu.VMEM((2, LEAF, LEAF), BF16),
            pltpu.VMEM((2, 2, LEAF, UPD), BF16),
            pltpu.VMEM((2, 2, PEERS, ROWS, LEAF), BF16),
            pltpu.VMEM((PEERS * SHARE, SHARE), BF16),
            pltpu.VMEM(trace, F32),
            pltpu.VMEM((2, 8, LEAF), F32),
            pltpu.VMEM((2, LEAF, 8), F32),
            *[pltpu.VMEM(trace, BF16) for _ in range(5)],
            *[pltpu.VMEM(trace, F32) for _ in range(5)],
            pltpu.VMEM((128, UPD), F32),
            pltpu.VMEM((128, SHARE), F32),
            pltpu.VMEM((SHARE, 128), F32),
            pltpu.VMEM((PEERS, ROWS, 128), F32),
            pltpu.VMEM((2, SHARE, 128), BF16),
            pltpu.VMEM((PEERS, ROWS, 128), BF16),
            pltpu.VMEM((4, SHARE, SHARE), BF16),
            pltpu.VMEM((PEERS, RHS, SHARE), BF16),
            pltpu.VMEM((SHARE, 128), BF16),
            pltpu.VMEM((PEERS, ROWS, 128), BF16),
            pltpu.SemaphoreType.DMA((8,)),
            pltpu.SemaphoreType.DMA((12,)),
            pltpu.SemaphoreType.DMA((12,)),
            *[pltpu.SemaphoreType.DMA((WAVES,)) for _ in range(4)],
            pltpu.SemaphoreType.DMA((8,)),
            pltpu.SemaphoreType.DMA((8,)),
            pltpu.SemaphoreType.DMA((PEERS,)),
            pltpu.SemaphoreType.DMA((PEERS,)),
        ],
        compiler_params=pltpu.CompilerParams(
            collective_id=0, has_side_effects=True, vmem_limit_bytes=56 * 1024 * 1024
        ),
        name="sweep",
    )(
        source_leaf[0], source_sep[0], leaf_inverse[0], lift[0], lower.reshape(2, PEERS, 2, ROWS, LEAF),
        sep_inverse[0], parent_map[0], couple_down[0], couple_up[0],
    )
    return leaf[None], sep[None]


def solution(mesh):
    return jax.shard_map(
        local,
        mesh=mesh,
        in_specs=(
            P("panel", "front", None, None),
            P("panel", None, "front"),
            P("panel", "front", None, None),
            P("panel", "front", None, None),
            P("panel", "front", None, None),
            P("panel", None, "front"),
            P("panel", "front", None),
            P("panel", "front", None),
            P("panel", "front", None),
        ),
        out_specs=(P("panel", "front", None, None), P("panel", None, "front")),
        check_vma=False,
    )
```

```python
import jax
import jax.numpy as jnp
from jax import lax
from jax.experimental import pallas as pl
from jax.experimental.pallas import tpu as pltpu
from jax.sharding import PartitionSpec as P

MESH = pl.DeviceIdType.MESH
F32 = jnp.float32
BF16 = jnp.bfloat16
LEAF = 1024
UPD = 512
SHARE = 256
RHS = 32
ROWS = 16
GROUP = 4
PEERS = 16
LAST = 7
DIRECT = 3
HALF = 16
WAVES = 4
CHUNK = 512
CHUNKS = LEAF // CHUNK

S_CP, S_SRC, S_A, S_LIFT, S_P, S_Q, S_UA, S_DA = 0, 1, 2, 4, 5, 7, 9, 10


def dot(a, b):
    return jnp.dot(a, b, preferred_element_type=F32)


def dot_t(a, b):
    return lax.dot_general(a, b, (((1,), (1,)), ((), ())), preferred_element_type=F32)


def kernel(
    src, ssep, inv, lift, lower, sepinv, pm, cd, cu,
    leaf_out, sep_out,
    A, PP, QQ, LL, LW, SS, SL, CP, CT,
    T, U, TS, US, DA, E, DB, G, UA, UB,
    Z, ZP, PMS, PMR, UPS, UPR, ONE, RED, PKS, PKR,
    lsem, ps, pr, dsnd, drcv, usnd, urcv, osnd, orcv, rsnd, rrcv,
):
    p = lax.axis_index("panel")
    me = lax.axis_index("front")
    core = lax.rem(p, 2)
    c = p // 2
    pair = (p + 1 - 2 * core, me)
    is0 = core == 0
    is1 = core == 1
    first = c == 0
    last = c == LAST
    def remote(s, d, ss, rs, dev):
        return pltpu.make_async_remote_copy(
            src_ref=s, dst_ref=d, send_sem=ss, recv_sem=rs, device_id=dev, device_id_type=MESH
        )

    def to_pair(s, d, i):
        return remote(s, d, ps.at[i], pr.at[i], pair)

    own = [pltpu.make_async_copy(inv.at[f], A.at[core, f], lsem.at[f]) for f in range(2)]
    own_lift = pltpu.make_async_copy(lift, LL.at[1], lsem.at[2])
    own_lower = [
        pltpu.make_async_copy(lower.at[f, :, h], LW.at[f, h], lsem.at[4 + 2 * f + h])
        for f in range(2)
        for h in range(2)
    ]
    own_sep = pltpu.make_async_copy(sepinv, SS, lsem.at[3])
    for copy in own:
        copy.start()

    barrier = pltpu.get_barrier_semaphore()

    def signal(dev):
        pl.semaphore_signal(barrier, inc=1, device_id=dev, device_id_type=MESH)

    @pl.when(is1)
    def _():
        @pl.when(c < LAST)
        def _():
            signal((p + 2, me))

        @pl.when(c > 0)
        def _():
            signal((p - 2, me))

        signal(pair)

    def greet(k, _):
        o = lax.rem(me + k, PEERS)

        @pl.when(k > 0)
        def _():
            signal((p, o))

        @pl.when(is0)
        def _():
            signal((p + 1, o))

        return 0

    lax.fori_loop(0, PEERS, greet, 0)
    CP[core, 0:2, :] = cd[...]
    CP[core, 2:4, :] = cu[...]
    Z[...] = jnp.zeros_like(Z)
    Z[0:2, :] = pm[...].astype(F32)
    Z[2:4, :] = pm[...].astype(F32)
    targets = Z[...].T.reshape(PEERS, 2, ROWS, 128)
    lane = lax.broadcasted_iota(jnp.int32, (PEERS, ROWS, 128), 2)
    PMS[...] = jnp.where(lane < 2, targets[:, 0], targets[:, 1]).reshape(PEERS * ROWS, 128)

    @pl.when(jnp.logical_and(is0, first))
    def _():
        for f in range(2):
            own[f].wait()
            DA[f] = dot(src[f].astype(BF16), A[0, f]).astype(BF16)

    ends = jnp.where(first, 0, 1) + jnp.where(last, 0, 1)
    far = PEERS + ends
    pl.semaphore_wait(barrier, PEERS - 1 + jnp.where(is1, far, 1))

    send_a = [to_pair(A.at[core, f], A.at[core, f], S_A + f) for f in range(2)]
    got_a = [to_pair(A.at[core, f], A.at[1 - core, f], S_A + f) for f in range(2)]

    def give_a():
        for f in range(2):

            @pl.when(jnp.logical_or(is1, c > 0))
            def _():
                own[f].wait()

            for half in range(2):
                rows = pl.ds(half * 512, 512)
                to_pair(A.at[core, f, rows], A.at[core, f, rows], S_A + f).start()

    send_cp = to_pair(CP.at[core], CP.at[core], S_CP)
    got_cp = to_pair(CP.at[core], CP.at[1 - core], S_CP)
    send_src = to_pair(src, SL, S_SRC)
    send_lift = to_pair(lift, LL.at[0], S_LIFT)
    ship_p = [to_pair(PP.at[f], PP.at[f], S_P + f) for f in range(2)]
    ship_q = [to_pair(QQ.at[f], QQ.at[f], S_Q + f) for f in range(2)]
    ship_ua = to_pair(UA, UA, S_UA)
    ship_da = [to_pair(DA.at[f], DA.at[f], S_DA + f) for f in range(2)]
    def part(k):
        return pl.ds(pl.multiple_of(k * ROWS, ROWS), ROWS)

    def to_owners(out, into, lane, target, to_self):
        def one(k, _):
            o = lax.rem(me + k, PEERS)
            remote(
                out.at[part(o)], into.at[me], osnd.at[lane], orcv.at[lane], (2 * c + target, o)
            ).start()
            return 0

        lax.fori_loop(0 if to_self else 1, PEERS, one, 0)
        if not to_self:
            into[me] = out[part(me), :]

    def several(ref, n, lane):
        some = ref.at[pl.ds(0, n)]
        return remote(some, some, osnd.at[lane], orcv.at[lane], pair)

    def send_targets():
        to_owners(PMS, PMR, 3, core, False)

    def build_maps():
        several(PMR, PEERS - 1, 3).wait()
        table = PMR[...].reshape(SHARE, 128)
        column = (lax.broadcasted_iota(jnp.int32, (SHARE, SHARE), 1) + me * SHARE).astype(F32)
        for q in range(4):
            ONE[q] = jnp.where(table[:, q : q + 1] == column, 1.0, 0.0).astype(BF16)

    def turned(ref):
        return ref[...].astype(F32).reshape(SHARE, 128).T.astype(BF16)

    def separator(x, swept):
        several(UPR, PEERS - x, 4 + x).wait_recv()
        updates = turned(UPR)
        gathered = jnp.zeros((RHS, SHARE), F32)
        for q in range(4):
            gathered += dot(updates[q * RHS : (q + 1) * RHS, :], ONE[q])
        RED[me] = (ssep[...] - gathered).astype(BF16)

        def spread(k):
            o = lax.rem(me + k, PEERS)
            return remote(RED.at[me], RED.at[me], rsnd.at[k], rrcv.at[k], (p, o))

        for k in range(1, PEERS):
            spread(k).start()
        own_sep.wait()
        total = jnp.zeros((RHS, SHARE), F32)
        for group in range(0, PEERS, GROUP):
            sources = [lax.rem(me + PEERS - k, PEERS) for k in range(group, group + GROUP)]
            for k, w in zip(range(group, group + GROUP), sources):
                if k:
                    remote(RED.at[w], RED.at[w], rsnd.at[k], rrcv.at[k], pair).wait_recv()
            for w in sources:
                total += dot(RED[w], SS[pl.ds(pl.multiple_of(w * SHARE, SHARE), SHARE), :])
        half = total.astype(BF16)
        for q in range(4):
            ZP[q * RHS : (q + 1) * RHS, :] = dot_t(half, ONE[q])
        PKS[...] = ZP[...].T.astype(BF16)
        to_owners(PKS, PKR, 6, x, False)
        sep_out[...] = total
        for copy in own_lower:
            copy.wait()
        if x == 0:
            ship_ua.wait_recv()
        several(PKR, PEERS - 1, 6).wait()
        picked = turned(PKR)
        for f in range(2):
            back = dot(picked[f * RHS : (f + 1) * RHS, :], LW[f, 0].reshape(SHARE, LEAF))
            back += dot(picked[(2 + f) * RHS : (3 + f) * RHS, :], LW[f, 1].reshape(SHARE, LEAF))
            leaf_out[f] = swept[f] - back
        for k in range(1, PEERS):
            spread(k).wait_send()

    @pl.when(is0)
    def _core0():
        @pl.when(first)
        def _():
            for copy in ship_da:
                copy.start()

        send_cp.start()
        send_src.start()
        give_a()
        send_targets()
        got_cp.wait_recv()
        for x in range(2):
            CT[x] = CP[x].T
        for f in range(2):
            got_a[f].wait_recv()

        @pl.when(c > DIRECT)
        def _():
            for f in range(2):

                @pl.loop(0, 4)
                def _(b):
                    rows = pl.ds(pl.multiple_of(b * 256, 256), 256)
                    left = (A[0, f, rows, :].astype(F32) * CP[1, f : f + 1, :]).astype(BF16)
                    PP[f, rows, :] = (dot(left, A[1, f]) * CT[0, rows, f : f + 1]).astype(BF16)
                    to_pair(PP.at[f, rows], PP.at[f, rows], S_P + f).start()

        for f in range(2):

            @pl.loop(0, 4)
            def _(b):
                rows = pl.ds(pl.multiple_of(b * 256, 256), 256)
                base = jnp.where(last, PP[f, rows, :].astype(F32), A[1, f, rows, :].astype(F32))
                left = (base * CP[0, f + 2 : f + 3, :]).astype(BF16)
                scale = jnp.where(last, 1.0, CT[1, rows, f + 2 : f + 3])
                extra = jnp.where(last, CT[0, rows, f : f + 1], 0.0)
                full = dot(left, A[0, f]) * scale + extra * A[0, f, rows, :].astype(F32)
                QQ[f, rows, :] = full.astype(BF16)
                to_pair(QQ.at[f, rows], QQ.at[f, rows], S_Q + f).start()

        send_lift.start()
        own_sep.start()
        for copy in own_lower:
            copy.start()
        build_maps()
        separator(0, UA)
        for copy in (send_cp, send_src, *send_a, send_lift, *ship_q):
            copy.wait_send()

        @pl.when(c > DIRECT)
        def _():
            for copy in ship_p:
                copy.wait_send()

        @pl.when(first)
        def _():
            for copy in ship_da:
                copy.wait_send()

    @pl.when(is1)
    def _core1():
        send_cp.start()
        give_a()
        send_targets()
        own_sep.start()
        own_lift.start()
        for copy in own_lower:
            copy.start()

        below = (p + 2, me)
        above = (p - 2, me)

        def down_wave(f, g, cols=slice(None)):
            rows, k = half_rows(g), 2 * f + g
            return remote(TS.at[f, rows, cols], T.at[f, rows, cols], dsnd.at[k], drcv.at[k], below)

        def up_wave(f, g, cols=slice(None)):
            rows, k = half_rows(g), 2 * f + g
            return remote(US.at[f, rows, cols], U.at[f, rows, cols], usnd.at[k], urcv.at[k], above)

        def half_rows(g):
            return pl.ds(pl.multiple_of(g * HALF, HALF), HALF)

        def coupled(x, f, k):
            return CP[x, pl.ds(f + k, 1), :]

        def each_wave(act):
            for w in range(WAVES):
                act(w // 2, w % 2)

        def waves(ready, left_of, weight, extra, keep, half, copy_of):
            def turn(i, _):
                w = i
                g = lax.rem(w, 2)
                f = w // 2
                rows = half_rows(g)

                ready(f, g)
                left = left_of(f, rows)
                parts = [slice(j * CHUNK, (j + 1) * CHUNK) for j in range(CHUNKS)]
                outs = []
                for cols in parts:
                    out = dot(left, weight[f, :, cols])
                    outs.append(out if extra is None else out + extra[f, rows, cols])
                for cols, out in zip(parts, outs):
                    half[f, rows, cols] = out.astype(BF16)
                    if copy_of is not None:
                        copy_of(f, g, cols).start()

                for cols, out in zip(parts, outs):
                    keep[f, rows, cols] = out
                return 0

            lax.fori_loop(0, WAVES, turn, 0)

        got_cp.wait_recv()

        @pl.when(first)
        def _():
            T[...] = jnp.zeros_like(T)

            def ready(f, g):
                @pl.when(g == 0)
                def _():
                    to_pair(DA.at[f], DA.at[f], S_DA + f).wait_recv()

            def left_of(f, rows):
                loaded = src[f, rows, :] + coupled(1, f, 0) * DA[f, rows, :].astype(F32)
                return loaded.astype(BF16)

            waves(ready, left_of, A.at[1], None, DB, TS, down_wave)
            send_src.wait_recv()
            for f in range(2):
                got_a[f].wait_recv()

        @pl.when(jnp.logical_and(c > 0, c <= DIRECT))
        def _():
            def ready(f, g):
                @pl.when(f + g == 0)
                def _():
                    send_src.wait_recv()

                @pl.when(g == 0)
                def _():
                    to_pair(A.at[core, f], A.at[1 - core, f], S_A + f).wait_recv()

                down_wave(f, g).wait_recv()

            def left_of(f, rows):
                loaded = SL[f, rows, :] + coupled(0, f, 0) * T[f, rows, :].astype(F32)
                middle = dot(loaded.astype(BF16), A[0, f])
                loaded = src[f, rows, :] + coupled(1, f, 0) * middle.astype(BF16).astype(F32)
                return loaded.astype(BF16)

            waves(ready, left_of, A.at[1], None, DB, TS, down_wave)

        @pl.when(c <= DIRECT)
        def _():
            build_maps()

        @pl.when(c > DIRECT)
        def _():
            send_src.wait_recv()
            for f in range(2):
                got_a[f].wait_recv()

            def alone(f, _):
                middle = dot(SL[f].astype(BF16), A[0, f])
                loaded = src[f] + coupled(1, f, 0) * middle.astype(BF16).astype(F32)
                out = dot(loaded.astype(BF16), A[1, f])
                DB[f] = out
                E[f] = out

                @pl.when(last)
                def _():
                    loaded = SL[f] + coupled(0, f, 2) * out.astype(BF16).astype(F32)
                    E[f] = dot(loaded.astype(BF16), A[0, f])

                return 0

            lax.fori_loop(0, 2, alone, 0)
            build_maps()

            def sweep(ship, weight, keep, half, copy_of):
                def ready(f, g):
                    @pl.when(g == 0)
                    def _():
                        to_pair(weight.at[f], weight.at[f], ship + f).wait_recv()

                    down_wave(f, g).wait_recv()

                waves(ready, lambda f, rows: T[f, rows, :], weight, E, keep, half, copy_of)

            @pl.when(c < LAST)
            def _():
                sweep(S_P, PP, DB, TS, down_wave)

            @pl.when(last)
            def _():
                sweep(S_Q, QQ, UA, US, up_wave)
                for f in range(2):
                    ship_p[f].wait_recv()

        @pl.when(c < LAST)
        def _():
            def before(f, _):
                loaded = (
                    SL[f]
                    + coupled(0, f, 0) * T[f].astype(F32)
                    + coupled(0, f, 2) * DB[f].astype(BF16).astype(F32)
                )
                G[f] = dot(loaded.astype(BF16), A[0, f])
                return 0

            lax.fori_loop(0, 2, before, 0)

            def ready(f, g):
                @pl.when(g == 0)
                def _():
                    to_pair(QQ.at[f], QQ.at[f], S_Q + f).wait_recv()

                up_wave(f, g).wait_recv()

            def left_of(f, rows):
                return U[f, rows, :]

            @pl.when(first)
            def _():
                waves(ready, left_of, QQ, G, UA, US, None)

            @pl.when(c > 0)
            def _():
                waves(ready, left_of, QQ, G, UA, US, up_wave)

        def lifted(x, half):
            for f in range(2):
                Z[f * RHS : (f + 1) * RHS, :] = dot(half[f], LL[x, f])
            rows = Z[0 : 2 * RHS, :].T.reshape(PEERS, 2, ROWS, 2 * RHS)
            packed = jnp.concatenate([rows[:, 0], rows[:, 1]], axis=-1)
            UPS[x] = packed.reshape(SHARE, 128).astype(BF16)
            to_owners(UPS.at[x], UPR, 4 + x, x, x == 0)

        send_lift.wait_recv()
        own_lift.wait()
        lifted(0, US)
        ship_ua.start()

        @pl.when(last)
        def _():
            def rest(f, _):
                UB[f] = DB[f] + dot(T[f], PP[f])
                return 0

            lax.fori_loop(0, 2, rest, 0)

        @pl.when(c < LAST)
        def _():
            def rest(f, _):
                loaded = coupled(1, f, 2) * U[f].astype(F32)
                UB[f] = DB[f] + dot(loaded.astype(BF16), A[1, f])
                return 0

            lax.fori_loop(0, 2, rest, 0)

        for f in range(2):
            DA[f] = UB[f].astype(BF16)
        lifted(1, DA)
        separator(1, UB)

        for copy in (send_cp, *send_a, ship_ua):
            copy.wait_send()
        several(UPR, PEERS, 4).wait_send()
        several(UPR, PEERS - 1, 5).wait_send()

        @pl.when(c < LAST)
        def _():
            each_wave(lambda f, g: down_wave(f, g).wait_send())

        @pl.when(c > 0)
        def _():
            each_wave(lambda f, g: up_wave(f, g).wait_send())


def hand_over(leaf, sep, leaf_out, sep_out):
    leaf_out[...] = leaf[...]
    sep_out[...] = sep[...]


def local(source_leaf, source_sep, leaf_inverse, lift, lower, sep_inverse, parent_map, couple_down, couple_up):
    vmem = pl.BlockSpec(memory_space=pltpu.VMEM)
    hbm = pl.BlockSpec(memory_space=pl.ANY)
    trace = (2, RHS, LEAF)
    leaf, sep = pl.pallas_call(
        kernel,
        out_shape=(
            jax.ShapeDtypeStruct(trace, F32),
            jax.ShapeDtypeStruct((RHS, SHARE), F32),
        ),
        in_specs=[vmem, vmem, hbm, hbm, hbm, hbm, vmem, vmem, vmem],
        out_specs=(vmem, vmem),
        scratch_shapes=[
            pltpu.VMEM((2, 2, LEAF, LEAF), BF16),
            pltpu.VMEM((2, LEAF, LEAF), BF16),
            pltpu.VMEM((2, LEAF, LEAF), BF16),
            pltpu.VMEM((2, 2, LEAF, UPD), BF16),
            pltpu.VMEM((2, 2, PEERS, ROWS, LEAF), BF16),
            pltpu.VMEM((PEERS * SHARE, SHARE), BF16),
            pltpu.VMEM(trace, F32),
            pltpu.VMEM((2, 8, LEAF), F32),
            pltpu.VMEM((2, LEAF, 8), F32),
            *[pltpu.VMEM(trace, BF16) for _ in range(5)],
            *[pltpu.VMEM(trace, F32) for _ in range(5)],
            pltpu.VMEM((128, UPD), F32),
            pltpu.VMEM((128, SHARE), F32),
            pltpu.VMEM((SHARE, 128), F32),
            pltpu.VMEM((PEERS, ROWS, 128), F32),
            pltpu.VMEM((2, SHARE, 128), BF16),
            pltpu.VMEM((PEERS, ROWS, 128), BF16),
            pltpu.VMEM((4, SHARE, SHARE), BF16),
            pltpu.VMEM((PEERS, RHS, SHARE), BF16),
            pltpu.VMEM((SHARE, 128), BF16),
            pltpu.VMEM((PEERS, ROWS, 128), BF16),
            pltpu.SemaphoreType.DMA((8,)),
            pltpu.SemaphoreType.DMA((12,)),
            pltpu.SemaphoreType.DMA((12,)),
            *[pltpu.SemaphoreType.DMA((WAVES,)) for _ in range(4)],
            pltpu.SemaphoreType.DMA((8,)),
            pltpu.SemaphoreType.DMA((8,)),
            pltpu.SemaphoreType.DMA((PEERS,)),
            pltpu.SemaphoreType.DMA((PEERS,)),
        ],
        compiler_params=pltpu.CompilerParams(
            collective_id=0, has_side_effects=True, vmem_limit_bytes=56 * 1024 * 1024
        ),
        name="sweep",
    )(
        source_leaf[0], source_sep[0], leaf_inverse[0], lift[0], lower.reshape(2, PEERS, 2, ROWS, LEAF),
        sep_inverse[0], parent_map[0], couple_down[0], couple_up[0],
    )
    leaf, sep = pl.pallas_call(
        hand_over,
        out_shape=(jax.ShapeDtypeStruct(trace, F32), jax.ShapeDtypeStruct((RHS, SHARE), F32)),
        in_specs=[vmem, vmem],
        out_specs=(vmem, vmem),
        name="hand_over",
    )(leaf, sep)
    return leaf[None], sep[None]


def solution(mesh):
    return jax.shard_map(
        local,
        mesh=mesh,
        in_specs=(
            P("panel", "front", None, None),
            P("panel", None, "front"),
            P("panel", "front", None, None),
            P("panel", "front", None, None),
            P("panel", "front", None, None),
            P("panel", None, "front"),
            P("panel", "front", None),
            P("panel", "front", None),
            P("panel", "front", None),
        ),
        out_specs=(P("panel", "front", None, None), P("panel", None, "front")),
        check_vma=False,
    )
```

```python
import jax
import jax.numpy as jnp
from jax import lax
from jax.experimental import pallas as pl
from jax.experimental.pallas import tpu as pltpu
from jax.sharding import PartitionSpec as P

MESH = pl.DeviceIdType.MESH
F32 = jnp.float32
BF16 = jnp.bfloat16
LEAF = 1024
UPD = 512
SHARE = 256
RHS = 32
ROWS = 16
GROUP = 4
PEERS = 16
LAST = 7
DIRECT = 3
HALF = 16
WAVES = 4
CHUNK = 512
CHUNKS = LEAF // CHUNK

S_CP, S_SRC, S_A, S_LIFT, S_P, S_Q, S_UA, S_DA = 0, 1, 2, 4, 5, 7, 9, 10


def dot(a, b):
    return jnp.dot(a, b, preferred_element_type=F32)


def dot_t(a, b):
    return lax.dot_general(a, b, (((1,), (1,)), ((), ())), preferred_element_type=F32)


def kernel(
    src, ssep, inv, lift, lower, sepinv, pm, cd, cu,
    leaf_out, sep_out,
    A, PP, QQ, LL, LW, SS, SL, CP, CT,
    T, U, TS, US, DA, E, DB, G, UA, UB,
    Z, ZP, PMS, PMR, UPS, UPR, ONE, RED, PKS, PKR,
    lsem, ps, pr, dsnd, drcv, usnd, urcv, osnd, orcv, rsnd, rrcv,
):
    p = lax.axis_index("panel")
    me = lax.axis_index("front")
    core = lax.rem(p, 2)
    c = p // 2
    pair = (p + 1 - 2 * core, me)
    is0 = core == 0
    is1 = core == 1
    first = c == 0
    last = c == LAST
    def remote(s, d, ss, rs, dev):
        return pltpu.make_async_remote_copy(
            src_ref=s, dst_ref=d, send_sem=ss, recv_sem=rs, device_id=dev, device_id_type=MESH
        )

    def to_pair(s, d, i):
        return remote(s, d, ps.at[i], pr.at[i], pair)

    own = [pltpu.make_async_copy(inv.at[f], A.at[core, f], lsem.at[f]) for f in range(2)]
    own_lift = pltpu.make_async_copy(lift, LL.at[1], lsem.at[2])
    own_lower = [
        pltpu.make_async_copy(lower.at[f, :, h], LW.at[f, h], lsem.at[4 + 2 * f + h])
        for f in range(2)
        for h in range(2)
    ]
    own_sep = pltpu.make_async_copy(sepinv, SS, lsem.at[3])
    for copy in own:
        copy.start()

    barrier = pltpu.get_barrier_semaphore()

    def signal(dev):
        pl.semaphore_signal(barrier, inc=1, device_id=dev, device_id_type=MESH)

    @pl.when(is1)
    def _():
        @pl.when(c < LAST)
        def _():
            signal((p + 2, me))

        @pl.when(c > 0)
        def _():
            signal((p - 2, me))

        signal(pair)

    def greet(k, _):
        o = lax.rem(me + k, PEERS)

        @pl.when(k > 0)
        def _():
            signal((p, o))

        @pl.when(is0)
        def _():
            signal((p + 1, o))

        return 0

    lax.fori_loop(0, PEERS, greet, 0)
    CP[core, 0:2, :] = cd[...]
    CP[core, 2:4, :] = cu[...]
    Z[...] = jnp.zeros_like(Z)
    Z[0:2, :] = pm[...].astype(F32)
    Z[2:4, :] = pm[...].astype(F32)
    targets = Z[...].T.reshape(PEERS, 2, ROWS, 128)
    lane = lax.broadcasted_iota(jnp.int32, (PEERS, ROWS, 128), 2)
    PMS[...] = jnp.where(lane < 2, targets[:, 0], targets[:, 1]).reshape(PEERS * ROWS, 128)

    @pl.when(jnp.logical_and(is0, first))
    def _():
        for f in range(2):
            own[f].wait()
            DA[f] = dot(src[f].astype(BF16), A[0, f]).astype(BF16)

    ends = jnp.where(first, 0, 1) + jnp.where(last, 0, 1)
    far = PEERS + ends
    pl.semaphore_wait(barrier, PEERS - 1 + jnp.where(is1, far, 1))

    send_a = [to_pair(A.at[core, f], A.at[core, f], S_A + f) for f in range(2)]
    got_a = [to_pair(A.at[core, f], A.at[1 - core, f], S_A + f) for f in range(2)]

    def give_a():
        for f in range(2):

            @pl.when(jnp.logical_or(is1, c > 0))
            def _():
                own[f].wait()

            for half in range(2):
                rows = pl.ds(half * 512, 512)
                to_pair(A.at[core, f, rows], A.at[core, f, rows], S_A + f).start()

    send_cp = to_pair(CP.at[core], CP.at[core], S_CP)
    got_cp = to_pair(CP.at[core], CP.at[1 - core], S_CP)
    send_src = to_pair(src, SL, S_SRC)
    send_lift = to_pair(lift, LL.at[0], S_LIFT)
    ship_p = [to_pair(PP.at[f], PP.at[f], S_P + f) for f in range(2)]
    ship_q = [to_pair(QQ.at[f], QQ.at[f], S_Q + f) for f in range(2)]
    ship_ua = to_pair(UA, UA, S_UA)
    ship_da = [to_pair(DA.at[f], DA.at[f], S_DA + f) for f in range(2)]
    def part(k):
        return pl.ds(pl.multiple_of(k * ROWS, ROWS), ROWS)

    def flipped(v, bits):
        return (v, v + 1 - 2 * lax.rem(v, 2), lax.rem(v + 2, 4), 3 - v)[bits]

    def across(k):
        return 4 * flipped(me // 4, k // 4) + flipped(lax.rem(me, 4), k % 4)

    far_first = range(PEERS - 1, 0, -1)

    def to_owners(out, into, lane, target, to_self):
        for k in (*far_first, *([0] if to_self else [])):
            o = across(k)
            remote(
                out.at[part(o)], into.at[me], osnd.at[lane], orcv.at[lane], (2 * c + target, o)
            ).start()
        if not to_self:
            into[me] = out[part(me), :]

    def several(ref, n, lane):
        some = ref.at[pl.ds(0, n)]
        return remote(some, some, osnd.at[lane], orcv.at[lane], pair)

    def send_targets():
        to_owners(PMS, PMR, 3, core, False)

    def build_maps():
        several(PMR, PEERS - 1, 3).wait()
        table = PMR[...].reshape(SHARE, 128)
        column = (lax.broadcasted_iota(jnp.int32, (SHARE, SHARE), 1) + me * SHARE).astype(F32)
        for q in range(4):
            ONE[q] = jnp.where(table[:, q : q + 1] == column, 1.0, 0.0).astype(BF16)

    def turned(ref):
        return ref[...].astype(F32).reshape(SHARE, 128).T.astype(BF16)

    def separator(x, swept):
        several(UPR, PEERS - x, 4 + x).wait_recv()
        updates = turned(UPR)
        gathered = jnp.zeros((RHS, SHARE), F32)
        for q in range(4):
            gathered += dot(updates[q * RHS : (q + 1) * RHS, :], ONE[q])
        RED[me] = (ssep[...] - gathered).astype(BF16)

        def spread(k):
            o = across(k)
            return remote(RED.at[me], RED.at[me], rsnd.at[k], rrcv.at[k], (p, o))

        for k in far_first:
            spread(k).start()
        own_sep.wait()
        total = jnp.zeros((RHS, SHARE), F32)
        for group in range(0, PEERS, GROUP):
            sources = [across(k) for k in range(group, group + GROUP)]
            for k, w in zip(range(group, group + GROUP), sources):
                if k:
                    remote(RED.at[w], RED.at[w], rsnd.at[k], rrcv.at[k], pair).wait_recv()
            for w in sources:
                total += dot(RED[w], SS[pl.ds(pl.multiple_of(w * SHARE, SHARE), SHARE), :])
        half = total.astype(BF16)
        for q in range(4):
            ZP[q * RHS : (q + 1) * RHS, :] = dot_t(half, ONE[q])
        PKS[...] = ZP[...].T.astype(BF16)
        to_owners(PKS, PKR, 6, x, False)
        sep_out[...] = total
        for copy in own_lower:
            copy.wait()
        if x == 0:
            ship_ua.wait_recv()
        several(PKR, PEERS - 1, 6).wait()
        picked = turned(PKR)
        for f in range(2):
            back = dot(picked[f * RHS : (f + 1) * RHS, :], LW[f, 0].reshape(SHARE, LEAF))
            back += dot(picked[(2 + f) * RHS : (3 + f) * RHS, :], LW[f, 1].reshape(SHARE, LEAF))
            leaf_out[f] = swept[f] - back
        for k in range(1, PEERS):
            spread(k).wait_send()

    @pl.when(is0)
    def _core0():
        @pl.when(first)
        def _():
            for copy in ship_da:
                copy.start()

        send_cp.start()
        send_src.start()
        give_a()
        send_targets()
        got_cp.wait_recv()
        for x in range(2):
            CT[x] = CP[x].T
        for f in range(2):
            got_a[f].wait_recv()

        @pl.when(c > DIRECT)
        def _():
            for f in range(2):

                @pl.loop(0, 4)
                def _(b):
                    rows = pl.ds(pl.multiple_of(b * 256, 256), 256)
                    left = (A[0, f, rows, :].astype(F32) * CP[1, f : f + 1, :]).astype(BF16)
                    PP[f, rows, :] = (dot(left, A[1, f]) * CT[0, rows, f : f + 1]).astype(BF16)
                    to_pair(PP.at[f, rows], PP.at[f, rows], S_P + f).start()

        for f in range(2):

            @pl.loop(0, 4)
            def _(b):
                rows = pl.ds(pl.multiple_of(b * 256, 256), 256)
                base = jnp.where(last, PP[f, rows, :].astype(F32), A[1, f, rows, :].astype(F32))
                left = (base * CP[0, f + 2 : f + 3, :]).astype(BF16)
                scale = jnp.where(last, 1.0, CT[1, rows, f + 2 : f + 3])
                extra = jnp.where(last, CT[0, rows, f : f + 1], 0.0)
                full = dot(left, A[0, f]) * scale + extra * A[0, f, rows, :].astype(F32)
                QQ[f, rows, :] = full.astype(BF16)
                to_pair(QQ.at[f, rows], QQ.at[f, rows], S_Q + f).start()

        send_lift.start()
        own_sep.start()
        for copy in own_lower:
            copy.start()
        build_maps()
        separator(0, UA)
        for copy in (send_cp, send_src, *send_a, send_lift, *ship_q):
            copy.wait_send()

        @pl.when(c > DIRECT)
        def _():
            for copy in ship_p:
                copy.wait_send()

        @pl.when(first)
        def _():
            for copy in ship_da:
                copy.wait_send()

    @pl.when(is1)
    def _core1():
        send_cp.start()
        give_a()
        send_targets()
        own_sep.start()
        own_lift.start()
        for copy in own_lower:
            copy.start()

        below = (p + 2, me)
        above = (p - 2, me)

        def down_wave(f, g, cols=slice(None)):
            rows, k = half_rows(g), 2 * f + g
            return remote(TS.at[f, rows, cols], T.at[f, rows, cols], dsnd.at[k], drcv.at[k], below)

        def up_wave(f, g, cols=slice(None)):
            rows, k = half_rows(g), 2 * f + g
            return remote(US.at[f, rows, cols], U.at[f, rows, cols], usnd.at[k], urcv.at[k], above)

        def half_rows(g):
            return pl.ds(pl.multiple_of(g * HALF, HALF), HALF)

        def coupled(x, f, k):
            return CP[x, pl.ds(f + k, 1), :]

        def each_wave(act):
            for w in range(WAVES):
                act(w // 2, w % 2)

        def waves(ready, left_of, weight, extra, keep, half, copy_of):
            def turn(i, _):
                w = i
                g = lax.rem(w, 2)
                f = w // 2
                rows = half_rows(g)

                ready(f, g)
                left = left_of(f, rows)
                parts = [slice(j * CHUNK, (j + 1) * CHUNK) for j in range(CHUNKS)]
                outs = []
                for cols in parts:
                    out = dot(left, weight[f, :, cols])
                    outs.append(out if extra is None else out + extra[f, rows, cols])
                for cols, out in zip(parts, outs):
                    half[f, rows, cols] = out.astype(BF16)
                    if copy_of is not None:
                        copy_of(f, g, cols).start()

                for cols, out in zip(parts, outs):
                    keep[f, rows, cols] = out
                return 0

            lax.fori_loop(0, WAVES, turn, 0)

        got_cp.wait_recv()

        @pl.when(first)
        def _():
            T[...] = jnp.zeros_like(T)

            def ready(f, g):
                @pl.when(g == 0)
                def _():
                    to_pair(DA.at[f], DA.at[f], S_DA + f).wait_recv()

            def left_of(f, rows):
                loaded = src[f, rows, :] + coupled(1, f, 0) * DA[f, rows, :].astype(F32)
                return loaded.astype(BF16)

            waves(ready, left_of, A.at[1], None, DB, TS, down_wave)
            send_src.wait_recv()
            for f in range(2):
                got_a[f].wait_recv()

        @pl.when(jnp.logical_and(c > 0, c <= DIRECT))
        def _():
            def ready(f, g):
                @pl.when(f + g == 0)
                def _():
                    send_src.wait_recv()

                @pl.when(g == 0)
                def _():
                    to_pair(A.at[core, f], A.at[1 - core, f], S_A + f).wait_recv()

                down_wave(f, g).wait_recv()

            def left_of(f, rows):
                loaded = SL[f, rows, :] + coupled(0, f, 0) * T[f, rows, :].astype(F32)
                middle = dot(loaded.astype(BF16), A[0, f])
                loaded = src[f, rows, :] + coupled(1, f, 0) * middle.astype(BF16).astype(F32)
                return loaded.astype(BF16)

            waves(ready, left_of, A.at[1], None, DB, TS, down_wave)

        @pl.when(c <= DIRECT)
        def _():
            build_maps()

        @pl.when(c > DIRECT)
        def _():
            send_src.wait_recv()
            for f in range(2):
                got_a[f].wait_recv()

            def alone(f, _):
                middle = dot(SL[f].astype(BF16), A[0, f])
                loaded = src[f] + coupled(1, f, 0) * middle.astype(BF16).astype(F32)
                out = dot(loaded.astype(BF16), A[1, f])
                DB[f] = out
                E[f] = out

                @pl.when(last)
                def _():
                    loaded = SL[f] + coupled(0, f, 2) * out.astype(BF16).astype(F32)
                    E[f] = dot(loaded.astype(BF16), A[0, f])

                return 0

            lax.fori_loop(0, 2, alone, 0)
            build_maps()

            def sweep(ship, weight, keep, half, copy_of):
                def ready(f, g):
                    @pl.when(g == 0)
                    def _():
                        to_pair(weight.at[f], weight.at[f], ship + f).wait_recv()

                    down_wave(f, g).wait_recv()

                waves(ready, lambda f, rows: T[f, rows, :], weight, E, keep, half, copy_of)

            @pl.when(c < LAST)
            def _():
                sweep(S_P, PP, DB, TS, down_wave)

            @pl.when(last)
            def _():
                sweep(S_Q, QQ, UA, US, up_wave)
                for f in range(2):
                    ship_p[f].wait_recv()

        @pl.when(c < LAST)
        def _():
            def before(f, _):
                loaded = (
                    SL[f]
                    + coupled(0, f, 0) * T[f].astype(F32)
                    + coupled(0, f, 2) * DB[f].astype(BF16).astype(F32)
                )
                G[f] = dot(loaded.astype(BF16), A[0, f])
                return 0

            lax.fori_loop(0, 2, before, 0)

            def ready(f, g):
                @pl.when(g == 0)
                def _():
                    to_pair(QQ.at[f], QQ.at[f], S_Q + f).wait_recv()

                up_wave(f, g).wait_recv()

            def left_of(f, rows):
                return U[f, rows, :]

            @pl.when(first)
            def _():
                waves(ready, left_of, QQ, G, UA, US, None)

            @pl.when(c > 0)
            def _():
                waves(ready, left_of, QQ, G, UA, US, up_wave)

        def lifted(x, half):
            for f in range(2):
                Z[f * RHS : (f + 1) * RHS, :] = dot(half[f], LL[x, f])
            rows = Z[0 : 2 * RHS, :].T.reshape(PEERS, 2, ROWS, 2 * RHS)
            packed = jnp.concatenate([rows[:, 0], rows[:, 1]], axis=-1)
            UPS[x] = packed.reshape(SHARE, 128).astype(BF16)
            to_owners(UPS.at[x], UPR, 4 + x, x, x == 0)

        send_lift.wait_recv()
        own_lift.wait()
        lifted(0, US)
        ship_ua.start()

        @pl.when(last)
        def _():
            def rest(f, _):
                UB[f] = DB[f] + dot(T[f], PP[f])
                return 0

            lax.fori_loop(0, 2, rest, 0)

        @pl.when(c < LAST)
        def _():
            def rest(f, _):
                loaded = coupled(1, f, 2) * U[f].astype(F32)
                UB[f] = DB[f] + dot(loaded.astype(BF16), A[1, f])
                return 0

            lax.fori_loop(0, 2, rest, 0)

        for f in range(2):
            DA[f] = UB[f].astype(BF16)
        lifted(1, DA)
        separator(1, UB)

        for copy in (send_cp, *send_a, ship_ua):
            copy.wait_send()
        several(UPR, PEERS, 4).wait_send()
        several(UPR, PEERS - 1, 5).wait_send()

        @pl.when(c < LAST)
        def _():
            each_wave(lambda f, g: down_wave(f, g).wait_send())

        @pl.when(c > 0)
        def _():
            each_wave(lambda f, g: up_wave(f, g).wait_send())


def hand_over(leaf, sep, leaf_out, sep_out, sem):
    copies = [
        pltpu.make_async_copy(leaf, leaf_out, sem.at[0]),
        pltpu.make_async_copy(sep, sep_out, sem.at[1]),
    ]
    for copy in copies:
        copy.start()
    for copy in copies:
        copy.wait()


def local(source_leaf, source_sep, leaf_inverse, lift, lower, sep_inverse, parent_map, couple_down, couple_up):
    vmem = pl.BlockSpec(memory_space=pltpu.VMEM)
    hbm = pl.BlockSpec(memory_space=pl.ANY)
    trace = (2, RHS, LEAF)
    leaf, sep = pl.pallas_call(
        kernel,
        out_shape=(pltpu.VMEM(trace, F32), pltpu.VMEM((RHS, SHARE), F32)),
        in_specs=[vmem, vmem, hbm, hbm, hbm, hbm, vmem, vmem, vmem],
        out_specs=(vmem, vmem),
        scratch_shapes=[
            pltpu.VMEM((2, 2, LEAF, LEAF), BF16),
            pltpu.VMEM((2, LEAF, LEAF), BF16),
            pltpu.VMEM((2, LEAF, LEAF), BF16),
            pltpu.VMEM((2, 2, LEAF, UPD), BF16),
            pltpu.VMEM((2, 2, PEERS, ROWS, LEAF), BF16),
            pltpu.VMEM((PEERS * SHARE, SHARE), BF16),
            pltpu.VMEM(trace, F32),
            pltpu.VMEM((2, 8, LEAF), F32),
            pltpu.VMEM((2, LEAF, 8), F32),
            *[pltpu.VMEM(trace, BF16) for _ in range(5)],
            *[pltpu.VMEM(trace, F32) for _ in range(5)],
            pltpu.VMEM((128, UPD), F32),
            pltpu.VMEM((128, SHARE), F32),
            pltpu.VMEM((SHARE, 128), F32),
            pltpu.VMEM((PEERS, ROWS, 128), F32),
            pltpu.VMEM((2, SHARE, 128), BF16),
            pltpu.VMEM((PEERS, ROWS, 128), BF16),
            pltpu.VMEM((4, SHARE, SHARE), BF16),
            pltpu.VMEM((PEERS, RHS, SHARE), BF16),
            pltpu.VMEM((SHARE, 128), BF16),
            pltpu.VMEM((PEERS, ROWS, 128), BF16),
            pltpu.SemaphoreType.DMA((8,)),
            pltpu.SemaphoreType.DMA((12,)),
            pltpu.SemaphoreType.DMA((12,)),
            *[pltpu.SemaphoreType.DMA((WAVES,)) for _ in range(4)],
            pltpu.SemaphoreType.DMA((8,)),
            pltpu.SemaphoreType.DMA((8,)),
            pltpu.SemaphoreType.DMA((PEERS,)),
            pltpu.SemaphoreType.DMA((PEERS,)),
        ],
        compiler_params=pltpu.CompilerParams(
            collective_id=0, has_side_effects=True, vmem_limit_bytes=56 * 1024 * 1024
        ),
        name="sweep",
    )(
        source_leaf[0], source_sep[0], leaf_inverse[0], lift[0], lower.reshape(2, PEERS, 2, ROWS, LEAF),
        sep_inverse[0], parent_map[0], couple_down[0], couple_up[0],
    )
    leaf, sep = pl.pallas_call(
        hand_over,
        out_shape=(jax.ShapeDtypeStruct(trace, F32), jax.ShapeDtypeStruct((RHS, SHARE), F32)),
        in_specs=[hbm, hbm],
        out_specs=(hbm, hbm),
        scratch_shapes=[pltpu.SemaphoreType.DMA((2,))],
        name="hand_over",
    )(
        pltpu.with_memory_space_constraint(leaf, pltpu.VMEM),
        pltpu.with_memory_space_constraint(sep, pltpu.VMEM),
    )
    return leaf[None], sep[None]


def solution(mesh):
    return jax.shard_map(
        local,
        mesh=mesh,
        in_specs=(
            P("panel", "front", None, None),
            P("panel", None, "front"),
            P("panel", "front", None, None),
            P("panel", "front", None, None),
            P("panel", "front", None, None),
            P("panel", None, "front"),
            P("panel", "front", None),
            P("panel", "front", None),
            P("panel", "front", None),
        ),
        out_specs=(P("panel", "front", None, None), P("panel", None, "front")),
        check_vma=False,
    )
```

```python
import jax
import jax.numpy as jnp
from jax import lax
from jax.experimental import pallas as pl
from jax.experimental.pallas import tpu as pltpu
from jax.sharding import PartitionSpec as P

MESH = pl.DeviceIdType.MESH
F32 = jnp.float32
BF16 = jnp.bfloat16
LEAF = 1024
UPD = 512
SHARE = 256
RHS = 32
ROWS = 16
GROUP = 4
PEERS = 16
LAST = 7
DIRECT = 3
HALF = 16
WAVES = 4
CHUNK = 512
CHUNKS = LEAF // CHUNK

S_CP, S_SRC, S_A, S_LIFT, S_P, S_Q, S_UA, S_DA = 0, 1, 2, 4, 5, 7, 9, 10


def dot(a, b):
    return jnp.dot(a, b, preferred_element_type=F32)


def dot_t(a, b):
    return lax.dot_general(a, b, (((1,), (1,)), ((), ())), preferred_element_type=F32)


def kernel(
    src, ssep, inv, lift, lower, sepinv, pm, cd, cu,
    leaf_out, sep_out,
    A, PP, QQ, LL, LW, SS, SL, CP, CT,
    T, U, TS, US, DA, E, DB, G, UA, UB,
    Z, ZP, PMS, PMR, UPS, UPR, ONE, RED, PKS, PKR,
    lsem, ps, pr, dsnd, drcv, usnd, urcv, osnd, orcv, rsnd, rrcv,
):
    p = lax.axis_index("panel")
    me = lax.axis_index("front")
    core = lax.rem(p, 2)
    c = p // 2
    pair = (p + 1 - 2 * core, me)
    is0 = core == 0
    is1 = core == 1
    first = c == 0
    second = c == 1
    last = c == LAST
    def remote(s, d, ss, rs, dev):
        return pltpu.make_async_remote_copy(
            src_ref=s, dst_ref=d, send_sem=ss, recv_sem=rs, device_id=dev, device_id_type=MESH
        )

    def to_pair(s, d, i):
        return remote(s, d, ps.at[i], pr.at[i], pair)

    own = [pltpu.make_async_copy(inv.at[f], A.at[core, f], lsem.at[f]) for f in range(2)]
    own_lift = pltpu.make_async_copy(lift, LL.at[1], lsem.at[2])
    own_lower = [
        pltpu.make_async_copy(lower.at[f, :, h], LW.at[f, h], lsem.at[4 + 2 * f + h])
        for f in range(2)
        for h in range(2)
    ]
    own_sep = pltpu.make_async_copy(sepinv, SS, lsem.at[3])
    for copy in own:
        copy.start()

    barrier = pltpu.get_barrier_semaphore()

    def signal(dev):
        pl.semaphore_signal(barrier, inc=1, device_id=dev, device_id_type=MESH)

    @pl.when(is1)
    def _():
        @pl.when(c < LAST)
        def _():
            signal((p + 2, me))

        @pl.when(c > 0)
        def _():
            signal((p - 2, me))

        signal(pair)

    @pl.when(jnp.logical_and(is0, second))
    def _():
        signal((p - 1, me))

    def greet(k, _):
        o = lax.rem(me + k, PEERS)

        @pl.when(k > 0)
        def _():
            signal((p, o))

        @pl.when(is0)
        def _():
            signal((p + 1, o))

        return 0

    lax.fori_loop(0, PEERS, greet, 0)
    CP[core, 0:2, :] = cd[...]
    CP[core, 2:4, :] = cu[...]
    Z[...] = jnp.zeros_like(Z)
    Z[0:2, :] = pm[...].astype(F32)
    Z[2:4, :] = pm[...].astype(F32)
    targets = Z[...].T.reshape(PEERS, 2, ROWS, 128)
    lane = lax.broadcasted_iota(jnp.int32, (PEERS, ROWS, 128), 2)
    PMS[...] = jnp.where(lane < 2, targets[:, 0], targets[:, 1]).reshape(PEERS * ROWS, 128)

    @pl.when(jnp.logical_and(is0, first))
    def _():
        for f in range(2):
            own[f].wait()
            DA[f] = dot(src[f].astype(BF16), A[0, f]).astype(BF16)

    ends = 1 + jnp.where(last, 0, 1)
    far = PEERS + ends
    pl.semaphore_wait(barrier, PEERS - 1 + jnp.where(is1, far, 1))

    send_a = [to_pair(A.at[core, f], A.at[core, f], S_A + f) for f in range(2)]
    got_a = [to_pair(A.at[core, f], A.at[1 - core, f], S_A + f) for f in range(2)]

    def give_front(f):
        for half in range(2):
            rows = pl.ds(half * 512, 512)
            to_pair(A.at[core, f, rows], A.at[core, f, rows], S_A + f).start()

    def give_a():
        for f in range(2):

            @pl.when(jnp.logical_or(is1, c > 0))
            def _():
                own[f].wait()

            if f == 0:
                give_front(0)
            else:

                @pl.when(jnp.logical_or(is1, jnp.logical_not(second)))
                def _():
                    give_front(1)

    send_cp = to_pair(CP.at[core], CP.at[core], S_CP)
    got_cp = to_pair(CP.at[core], CP.at[1 - core], S_CP)
    send_src = to_pair(src, SL, S_SRC)
    send_lift = to_pair(lift, LL.at[0], S_LIFT)
    ship_p = [to_pair(PP.at[f], PP.at[f], S_P + f) for f in range(2)]
    ship_q = [to_pair(QQ.at[f], QQ.at[f], S_Q + f) for f in range(2)]
    ship_ua = to_pair(UA, UA, S_UA)
    ship_da = [to_pair(DA.at[f], DA.at[f], S_DA + f) for f in range(2)]
    def side_wave(g, cols=slice(None)):
        rows = pl.ds(pl.multiple_of(g * HALF, HALF), HALF)
        return remote(TS.at[1, rows, cols], T.at[1, rows, cols], osnd.at[g], orcv.at[g], (p + 1, me))

    def ship_middle(g):
        rows = pl.ds(g * HALF, HALF)
        return to_pair(DA.at[1, rows], DA.at[1, rows], S_DA + g)

    def part(k):
        return pl.ds(pl.multiple_of(k * ROWS, ROWS), ROWS)

    def flipped(v, bits):
        return (v, v + 1 - 2 * lax.rem(v, 2), lax.rem(v + 2, 4), 3 - v)[bits]

    def across(k):
        return 4 * flipped(me // 4, k // 4) + flipped(lax.rem(me, 4), k % 4)

    far_first = range(PEERS - 1, 0, -1)

    def to_owners(out, into, lane, target, to_self):
        for k in (*far_first, *([0] if to_self else [])):
            o = across(k)
            remote(
                out.at[part(o)], into.at[me], osnd.at[lane], orcv.at[lane], (2 * c + target, o)
            ).start()
        if not to_self:
            into[me] = out[part(me), :]

    def several(ref, n, lane):
        some = ref.at[pl.ds(0, n)]
        return remote(some, some, osnd.at[lane], orcv.at[lane], pair)

    def send_targets():
        to_owners(PMS, PMR, 3, core, False)

    def build_maps():
        several(PMR, PEERS - 1, 3).wait()
        table = PMR[...].reshape(SHARE, 128)
        column = (lax.broadcasted_iota(jnp.int32, (SHARE, SHARE), 1) + me * SHARE).astype(F32)
        for q in range(4):
            ONE[q] = jnp.where(table[:, q : q + 1] == column, 1.0, 0.0).astype(BF16)

    def turned(ref):
        return ref[...].astype(F32).reshape(SHARE, 128).T.astype(BF16)

    def separator(x, swept):
        several(UPR, PEERS - x, 4 + x).wait_recv()
        updates = turned(UPR)
        gathered = jnp.zeros((RHS, SHARE), F32)
        for q in range(4):
            gathered += dot(updates[q * RHS : (q + 1) * RHS, :], ONE[q])
        RED[me] = (ssep[...] - gathered).astype(BF16)

        def spread(k):
            o = across(k)
            return remote(RED.at[me], RED.at[me], rsnd.at[k], rrcv.at[k], (p, o))

        for k in far_first:
            spread(k).start()
        own_sep.wait()
        total = jnp.zeros((RHS, SHARE), F32)
        for group in range(0, PEERS, GROUP):
            sources = [across(k) for k in range(group, group + GROUP)]
            for k, w in zip(range(group, group + GROUP), sources):
                if k:
                    remote(RED.at[w], RED.at[w], rsnd.at[k], rrcv.at[k], pair).wait_recv()
            for w in sources:
                total += dot(RED[w], SS[pl.ds(pl.multiple_of(w * SHARE, SHARE), SHARE), :])
        half = total.astype(BF16)
        for q in range(4):
            ZP[q * RHS : (q + 1) * RHS, :] = dot_t(half, ONE[q])
        PKS[...] = ZP[...].T.astype(BF16)
        to_owners(PKS, PKR, 6, x, False)
        sep_out[...] = total
        for copy in own_lower:
            copy.wait()
        if x == 0:
            ship_ua.wait_recv()
        several(PKR, PEERS - 1, 6).wait()
        picked = turned(PKR)
        for f in range(2):
            back = dot(picked[f * RHS : (f + 1) * RHS, :], LW[f, 0].reshape(SHARE, LEAF))
            back += dot(picked[(2 + f) * RHS : (3 + f) * RHS, :], LW[f, 1].reshape(SHARE, LEAF))
            leaf_out[f] = swept[f] - back
        for k in range(1, PEERS):
            spread(k).wait_send()

    @pl.when(is0)
    def _core0():
        @pl.when(first)
        def _():
            for copy in ship_da:
                copy.start()

        send_cp.start()
        send_src.start()
        give_a()
        send_targets()
        @pl.when(second)
        def _():
            for g in range(2):
                rows = slice(g * HALF, (g + 1) * HALF)
                side_wave(g).wait_recv()
                loaded = src[1, rows, :] + CP[0, 1:2, :] * T[1, rows, :].astype(F32)
                DA[1, rows, :] = dot(loaded.astype(BF16), A[0, 1]).astype(BF16)
                ship_middle(g).start()
            give_front(1)

        got_cp.wait_recv()
        for x in range(2):
            CT[x] = CP[x].T
        for f in range(2):
            got_a[f].wait_recv()

        @pl.when(c > DIRECT)
        def _():
            for f in range(2):

                @pl.loop(0, 4)
                def _(b):
                    rows = pl.ds(pl.multiple_of(b * 256, 256), 256)
                    left = (A[0, f, rows, :].astype(F32) * CP[1, f : f + 1, :]).astype(BF16)
                    PP[f, rows, :] = (dot(left, A[1, f]) * CT[0, rows, f : f + 1]).astype(BF16)
                    to_pair(PP.at[f, rows], PP.at[f, rows], S_P + f).start()

        for f in range(2):

            @pl.loop(0, 4)
            def _(b):
                rows = pl.ds(pl.multiple_of(b * 256, 256), 256)
                base = jnp.where(last, PP[f, rows, :].astype(F32), A[1, f, rows, :].astype(F32))
                left = (base * CP[0, f + 2 : f + 3, :]).astype(BF16)
                scale = jnp.where(last, 1.0, CT[1, rows, f + 2 : f + 3])
                extra = jnp.where(last, CT[0, rows, f : f + 1], 0.0)
                full = dot(left, A[0, f]) * scale + extra * A[0, f, rows, :].astype(F32)
                QQ[f, rows, :] = full.astype(BF16)
                to_pair(QQ.at[f, rows], QQ.at[f, rows], S_Q + f).start()

        send_lift.start()
        own_sep.start()
        for copy in own_lower:
            copy.start()
        build_maps()
        separator(0, UA)
        for copy in (send_cp, send_src, *send_a, send_lift, *ship_q):
            copy.wait_send()

        @pl.when(c > DIRECT)
        def _():
            for copy in ship_p:
                copy.wait_send()

        @pl.when(first)
        def _():
            for copy in ship_da:
                copy.wait_send()

        @pl.when(second)
        def _():
            for g in range(2):
                ship_middle(g).wait_send()

    @pl.when(is1)
    def _core1():
        send_cp.start()
        give_a()
        send_targets()
        own_sep.start()
        own_lift.start()
        for copy in own_lower:
            copy.start()

        below = (p + 2, me)
        above = (p - 2, me)

        def down_wave(f, g, cols=slice(None)):
            rows, k = half_rows(g), 2 * f + g
            return remote(TS.at[f, rows, cols], T.at[f, rows, cols], dsnd.at[k], drcv.at[k], below)

        def up_wave(f, g, cols=slice(None)):
            rows, k = half_rows(g), 2 * f + g
            return remote(US.at[f, rows, cols], U.at[f, rows, cols], usnd.at[k], urcv.at[k], above)

        def send_down(f, g, cols):
            down_wave(f, g, cols).start()

        def send_up(f, g, cols):
            up_wave(f, g, cols).start()

        def half_rows(g):
            return pl.ds(pl.multiple_of(g * HALF, HALF), HALF)

        def coupled(x, f, k):
            return CP[x, pl.ds(f + k, 1), :]

        def each_wave(act):
            for w in range(WAVES):
                act(w // 2, w % 2)

        def waves(ready, left_of, weight, extra, keep, half, copy_of, begin=0, end=WAVES):
            def turn(i, _):
                w = i
                g = lax.rem(w, 2)
                f = w // 2
                rows = half_rows(g)

                ready(f, g)
                left = left_of(f, rows)
                parts = [slice(j * CHUNK, (j + 1) * CHUNK) for j in range(CHUNKS)]
                outs = []
                for cols in parts:
                    out = dot(left, weight[f, :, cols])
                    outs.append(out if extra is None else out + extra[f, rows, cols])
                for cols, out in zip(parts, outs):
                    half[f, rows, cols] = out.astype(BF16)
                    if copy_of is not None:
                        copy_of(f, g, cols)

                for cols, out in zip(parts, outs):
                    keep[f, rows, cols] = out
                return 0

            lax.fori_loop(begin, end, turn, 0)

        def left_of_middle(f, rows):
            loaded = src[f, rows, :] + coupled(1, f, 0) * DA[f, rows, :].astype(F32)
            return loaded.astype(BF16)

        got_cp.wait_recv()

        @pl.when(first)
        def _():
            T[...] = jnp.zeros_like(T)

            def ready(f, g):
                @pl.when(g == 0)
                def _():
                    to_pair(DA.at[f], DA.at[f], S_DA + f).wait_recv()

            def send_first(f, g, cols):
                @pl.when(f == 1)
                def _():
                    side_wave(g, cols).start()

                send_down(f, g, cols)

            waves(ready, left_of_middle, A.at[1], None, DB, TS, send_first)
            send_src.wait_recv()
            for f in range(2):
                got_a[f].wait_recv()

        @pl.when(jnp.logical_and(c > 0, c <= DIRECT))
        def _():
            def ready(f, g):
                @pl.when(f + g == 0)
                def _():
                    send_src.wait_recv()

                @pl.when(g == 0)
                def _():
                    to_pair(A.at[core, f], A.at[1 - core, f], S_A + f).wait_recv()

                down_wave(f, g).wait_recv()

            def left_of(f, rows):
                loaded = SL[f, rows, :] + coupled(0, f, 0) * T[f, rows, :].astype(F32)
                middle = dot(loaded.astype(BF16), A[0, f])
                loaded = src[f, rows, :] + coupled(1, f, 0) * middle.astype(BF16).astype(F32)
                return loaded.astype(BF16)

            @pl.when(second)
            def _():
                waves(ready, left_of, A.at[1], None, DB, TS, send_down, 0, 2)

                def ready_middle(f, g):
                    to_pair(DA.at[1, half_rows(g)], DA.at[1, half_rows(g)], S_DA + g).wait_recv()

                waves(ready_middle, left_of_middle, A.at[1], None, DB, TS, send_down, 2, 4)
                got_a[1].wait_recv()
                for g in range(2):
                    down_wave(1, g).wait_recv()

            @pl.when(c > 1)
            def _():
                waves(ready, left_of, A.at[1], None, DB, TS, send_down)


        @pl.when(c <= DIRECT)
        def _():
            build_maps()

        @pl.when(c > DIRECT)
        def _():
            send_src.wait_recv()
            for f in range(2):
                got_a[f].wait_recv()

            def alone(f, _):
                middle = dot(SL[f].astype(BF16), A[0, f])
                loaded = src[f] + coupled(1, f, 0) * middle.astype(BF16).astype(F32)
                out = dot(loaded.astype(BF16), A[1, f])
                DB[f] = out
                E[f] = out

                @pl.when(last)
                def _():
                    loaded = SL[f] + coupled(0, f, 2) * out.astype(BF16).astype(F32)
                    E[f] = dot(loaded.astype(BF16), A[0, f])

                return 0

            lax.fori_loop(0, 2, alone, 0)
            build_maps()

            def sweep(ship, weight, keep, half, copy_of):
                def ready(f, g):
                    @pl.when(g == 0)
                    def _():
                        to_pair(weight.at[f], weight.at[f], ship + f).wait_recv()

                    down_wave(f, g).wait_recv()

                waves(ready, lambda f, rows: T[f, rows, :], weight, E, keep, half, copy_of)

            @pl.when(c < LAST)
            def _():
                sweep(S_P, PP, DB, TS, send_down)

            @pl.when(last)
            def _():
                sweep(S_Q, QQ, UA, US, send_up)
                for f in range(2):
                    ship_p[f].wait_recv()

        @pl.when(c < LAST)
        def _():
            def before(f, _):
                loaded = (
                    SL[f]
                    + coupled(0, f, 0) * T[f].astype(F32)
                    + coupled(0, f, 2) * DB[f].astype(BF16).astype(F32)
                )
                G[f] = dot(loaded.astype(BF16), A[0, f])
                return 0

            lax.fori_loop(0, 2, before, 0)

            def ready(f, g):
                @pl.when(g == 0)
                def _():
                    to_pair(QQ.at[f], QQ.at[f], S_Q + f).wait_recv()

                up_wave(f, g).wait_recv()

            def left_of(f, rows):
                return U[f, rows, :]

            @pl.when(first)
            def _():
                waves(ready, left_of, QQ, G, UA, US, None)

            @pl.when(c > 0)
            def _():
                waves(ready, left_of, QQ, G, UA, US, send_up)

        def lifted(x, half):
            for f in range(2):
                Z[f * RHS : (f + 1) * RHS, :] = dot(half[f], LL[x, f])
            rows = Z[0 : 2 * RHS, :].T.reshape(PEERS, 2, ROWS, 2 * RHS)
            packed = jnp.concatenate([rows[:, 0], rows[:, 1]], axis=-1)
            UPS[x] = packed.reshape(SHARE, 128).astype(BF16)
            to_owners(UPS.at[x], UPR, 4 + x, x, x == 0)

        send_lift.wait_recv()
        own_lift.wait()
        lifted(0, US)
        ship_ua.start()

        @pl.when(last)
        def _():
            def rest(f, _):
                UB[f] = DB[f] + dot(T[f], PP[f])
                return 0

            lax.fori_loop(0, 2, rest, 0)

        @pl.when(c < LAST)
        def _():
            def rest(f, _):
                loaded = coupled(1, f, 2) * U[f].astype(F32)
                UB[f] = DB[f] + dot(loaded.astype(BF16), A[1, f])
                return 0

            lax.fori_loop(0, 2, rest, 0)

        for f in range(2):
            DA[f] = UB[f].astype(BF16)
        lifted(1, DA)
        separator(1, UB)

        for copy in (send_cp, *send_a, ship_ua):
            copy.wait_send()
        several(UPR, PEERS, 4).wait_send()
        several(UPR, PEERS - 1, 5).wait_send()

        @pl.when(c < LAST)
        def _():
            each_wave(lambda f, g: down_wave(f, g).wait_send())

        @pl.when(first)
        def _():
            for g in range(2):
                side_wave(g).wait_send()

        @pl.when(c > 0)
        def _():
            each_wave(lambda f, g: up_wave(f, g).wait_send())


def hand_over(leaf, sep, leaf_out, sep_out, sem):
    copies = [
        pltpu.make_async_copy(leaf, leaf_out, sem.at[0]),
        pltpu.make_async_copy(sep, sep_out, sem.at[1]),
    ]
    for copy in copies:
        copy.start()
    for copy in copies:
        copy.wait()


def local(source_leaf, source_sep, leaf_inverse, lift, lower, sep_inverse, parent_map, couple_down, couple_up):
    vmem = pl.BlockSpec(memory_space=pltpu.VMEM)
    hbm = pl.BlockSpec(memory_space=pl.ANY)
    trace = (2, RHS, LEAF)
    leaf, sep = pl.pallas_call(
        kernel,
        out_shape=(pltpu.VMEM(trace, F32), pltpu.VMEM((RHS, SHARE), F32)),
        in_specs=[vmem, vmem, hbm, hbm, hbm, hbm, vmem, vmem, vmem],
        out_specs=(vmem, vmem),
        scratch_shapes=[
            pltpu.VMEM((2, 2, LEAF, LEAF), BF16),
            pltpu.VMEM((2, LEAF, LEAF), BF16),
            pltpu.VMEM((2, LEAF, LEAF), BF16),
            pltpu.VMEM((2, 2, LEAF, UPD), BF16),
            pltpu.VMEM((2, 2, PEERS, ROWS, LEAF), BF16),
            pltpu.VMEM((PEERS * SHARE, SHARE), BF16),
            pltpu.VMEM(trace, F32),
            pltpu.VMEM((2, 8, LEAF), F32),
            pltpu.VMEM((2, LEAF, 8), F32),
            *[pltpu.VMEM(trace, BF16) for _ in range(5)],
            *[pltpu.VMEM(trace, F32) for _ in range(5)],
            pltpu.VMEM((128, UPD), F32),
            pltpu.VMEM((128, SHARE), F32),
            pltpu.VMEM((SHARE, 128), F32),
            pltpu.VMEM((PEERS, ROWS, 128), F32),
            pltpu.VMEM((2, SHARE, 128), BF16),
            pltpu.VMEM((PEERS, ROWS, 128), BF16),
            pltpu.VMEM((4, SHARE, SHARE), BF16),
            pltpu.VMEM((PEERS, RHS, SHARE), BF16),
            pltpu.VMEM((SHARE, 128), BF16),
            pltpu.VMEM((PEERS, ROWS, 128), BF16),
            pltpu.SemaphoreType.DMA((8,)),
            pltpu.SemaphoreType.DMA((12,)),
            pltpu.SemaphoreType.DMA((12,)),
            *[pltpu.SemaphoreType.DMA((WAVES,)) for _ in range(4)],
            pltpu.SemaphoreType.DMA((8,)),
            pltpu.SemaphoreType.DMA((8,)),
            pltpu.SemaphoreType.DMA((PEERS,)),
            pltpu.SemaphoreType.DMA((PEERS,)),
        ],
        compiler_params=pltpu.CompilerParams(
            collective_id=0, has_side_effects=True, vmem_limit_bytes=56 * 1024 * 1024
        ),
        name="sweep",
    )(
        source_leaf[0], source_sep[0], leaf_inverse[0], lift[0], lower.reshape(2, PEERS, 2, ROWS, LEAF),
        sep_inverse[0], parent_map[0], couple_down[0], couple_up[0],
    )
    leaf, sep = pl.pallas_call(
        hand_over,
        out_shape=(jax.ShapeDtypeStruct(trace, F32), jax.ShapeDtypeStruct((RHS, SHARE), F32)),
        in_specs=[hbm, hbm],
        out_specs=(hbm, hbm),
        scratch_shapes=[pltpu.SemaphoreType.DMA((2,))],
        name="hand_over",
    )(
        pltpu.with_memory_space_constraint(leaf, pltpu.VMEM),
        pltpu.with_memory_space_constraint(sep, pltpu.VMEM),
    )
    return leaf[None], sep[None]


def solution(mesh):
    return jax.shard_map(
        local,
        mesh=mesh,
        in_specs=(
            P("panel", "front", None, None),
            P("panel", None, "front"),
            P("panel", "front", None, None),
            P("panel", "front", None, None),
            P("panel", "front", None, None),
            P("panel", None, "front"),
            P("panel", "front", None),
            P("panel", "front", None),
            P("panel", "front", None),
        ),
        out_specs=(P("panel", "front", None, None), P("panel", None, "front")),
        check_vma=False,
    )
```

```python
import jax
import jax.numpy as jnp
from jax import lax
from jax.experimental import pallas as pl
from jax.experimental.pallas import tpu as pltpu
from jax.sharding import PartitionSpec as P

MESH = pl.DeviceIdType.MESH
F32 = jnp.float32
BF16 = jnp.bfloat16
LEAF = 1024
UPD = 512
SHARE = 256
RHS = 32
ROWS = 16
GROUP = 4
PEERS = 16
LAST = 7
DIRECT = 3
HALF = 16
WAVES = 4
CHUNK = 512
CHUNKS = LEAF // CHUNK

S_CP, S_SRC, S_A, S_LIFT, S_P, S_Q, S_UA, S_DA = 0, 1, 2, 4, 5, 7, 9, 10


def dot(a, b):
    return jnp.dot(a, b, preferred_element_type=F32)


def dot_t(a, b):
    return lax.dot_general(a, b, (((1,), (1,)), ((), ())), preferred_element_type=F32)


def kernel(
    src, ssep, inv, lift, lower, sepinv, pm, cd, cu,
    leaf_out, sep_out,
    A, PP, QQ, LL, LW, SS, SL, CP, CT,
    T, U, TS, US, DA, E, DB, G, UA, UB,
    NL, QL, DL, GL, Z, ZP, PMS, PMR, UPS, UPR, ONE, RED, PKS, PKR,
    lsem, ps, pr, dsnd, drcv, usnd, urcv, osnd, orcv, rsnd, rrcv,
):
    p = lax.axis_index("panel")
    me = lax.axis_index("front")
    core = lax.rem(p, 2)
    c = p // 2
    pair = (p + 1 - 2 * core, me)
    is0 = core == 0
    is1 = core == 1
    first = c == 0
    second = c == 1
    last = c == LAST
    def remote(s, d, ss, rs, dev):
        return pltpu.make_async_remote_copy(
            src_ref=s, dst_ref=d, send_sem=ss, recv_sem=rs, device_id=dev, device_id_type=MESH
        )

    def to_pair(s, d, i):
        return remote(s, d, ps.at[i], pr.at[i], pair)

    own = [pltpu.make_async_copy(inv.at[f], A.at[core, f], lsem.at[f]) for f in range(2)]
    own_lift = pltpu.make_async_copy(lift, LL.at[1], lsem.at[2])
    own_lower = [
        pltpu.make_async_copy(lower.at[f, :, h], LW.at[f, h], lsem.at[4 + 2 * f + h])
        for f in range(2)
        for h in range(2)
    ]
    own_sep = pltpu.make_async_copy(sepinv, SS, lsem.at[3])
    for copy in own:
        copy.start()

    barrier = pltpu.get_barrier_semaphore()

    def signal(dev):
        pl.semaphore_signal(barrier, inc=1, device_id=dev, device_id_type=MESH)

    @pl.when(is1)
    def _():
        @pl.when(c < LAST)
        def _():
            signal((p + 2, me))

        @pl.when(c > 0)
        def _():
            signal((p - 2, me))

        signal(pair)

    @pl.when(jnp.logical_and(is0, second))
    def _():
        signal((p - 1, me))

    def greet(k, _):
        o = lax.rem(me + k, PEERS)

        @pl.when(k > 0)
        def _():
            signal((p, o))

        @pl.when(is0)
        def _():
            signal((p + 1, o))

        return 0

    lax.fori_loop(0, PEERS, greet, 0)
    CP[core, 0:2, :] = cd[...]
    CP[core, 2:4, :] = cu[...]
    Z[...] = jnp.zeros_like(Z)
    Z[0:2, :] = pm[...].astype(F32)
    Z[2:4, :] = pm[...].astype(F32)
    targets = Z[...].T.reshape(PEERS, 2, ROWS, 128)
    lane = lax.broadcasted_iota(jnp.int32, (PEERS, ROWS, 128), 2)
    PMS[...] = jnp.where(lane < 2, targets[:, 0], targets[:, 1]).reshape(PEERS * ROWS, 128)

    @pl.when(jnp.logical_and(is0, first))
    def _():
        for f in range(2):
            own[f].wait()
            DA[f] = dot(src[f].astype(BF16), A[0, f]).astype(BF16)

    ends = 1 + jnp.where(last, 0, 1)
    far = PEERS + ends
    pl.semaphore_wait(barrier, PEERS - 1 + jnp.where(is1, far, 1))

    send_a = [to_pair(A.at[core, f], A.at[core, f], S_A + f) for f in range(2)]
    got_a = [to_pair(A.at[core, f], A.at[1 - core, f], S_A + f) for f in range(2)]

    def give_front(f):
        for half in range(2):
            rows = pl.ds(half * 512, 512)
            to_pair(A.at[core, f, rows], A.at[core, f, rows], S_A + f).start()

    def give_a():
        for f in range(2):

            @pl.when(jnp.logical_or(is1, c > 0))
            def _():
                own[f].wait()

            if f == 0:
                give_front(0)
            else:

                @pl.when(jnp.logical_or(is1, jnp.logical_not(second)))
                def _():
                    give_front(1)

    send_cp = to_pair(CP.at[core], CP.at[core], S_CP)
    got_cp = to_pair(CP.at[core], CP.at[1 - core], S_CP)
    send_src = to_pair(src, SL, S_SRC)
    send_lift = to_pair(lift, LL.at[0], S_LIFT)
    ship_p = [to_pair(PP.at[f], PP.at[f], S_P + f) for f in range(2)]
    ship_q = [to_pair(QQ.at[f], QQ.at[f], S_Q + f) for f in range(2)]
    ship_ua = to_pair(UA, UA, S_UA)
    ship_da = [to_pair(DA.at[f], DA.at[f], S_DA + f) for f in range(2)]
    def side_wave(g, cols=slice(None)):
        rows = pl.ds(pl.multiple_of(g * HALF, HALF), HALF)
        return remote(TS.at[1, rows, cols], T.at[1, rows, cols], osnd.at[g], orcv.at[g], (p + 1, me))

    def ship_middle(g):
        rows = pl.ds(g * HALF, HALF)
        return to_pair(DA.at[1, rows], DA.at[1, rows], S_DA + g)

    def part(k):
        return pl.ds(pl.multiple_of(k * ROWS, ROWS), ROWS)

    def flipped(v, bits):
        return (v, v + 1 - 2 * lax.rem(v, 2), lax.rem(v + 2, 4), 3 - v)[bits]

    def across(k):
        return 4 * flipped(me // 4, k // 4) + flipped(lax.rem(me, 4), k % 4)

    far_first = range(PEERS - 1, 0, -1)

    def to_owners(out, into, lane, target, to_self):
        for k in (*far_first, *([0] if to_self else [])):
            o = across(k)
            remote(
                out.at[part(o)], into.at[me], osnd.at[lane], orcv.at[lane], (2 * c + target, o)
            ).start()
        if not to_self:
            into[me] = out[part(me), :]

    def several(ref, n, lane):
        some = ref.at[pl.ds(0, n)]
        return remote(some, some, osnd.at[lane], orcv.at[lane], pair)

    def send_targets():
        to_owners(PMS, PMR, 3, core, False)

    def build_maps():
        several(PMR, PEERS - 1, 3).wait()
        table = PMR[...].reshape(SHARE, 128)
        column = (lax.broadcasted_iota(jnp.int32, (SHARE, SHARE), 1) + me * SHARE).astype(F32)
        for q in range(4):
            ONE[q] = jnp.where(table[:, q : q + 1] == column, 1.0, 0.0).astype(BF16)

    def turned(ref):
        return ref[...].astype(F32).reshape(SHARE, 128).T.astype(BF16)

    def separator(x, swept):
        several(UPR, PEERS - x, 4 + x).wait_recv()
        updates = turned(UPR)
        gathered = jnp.zeros((RHS, SHARE), F32)
        for q in range(4):
            gathered += dot(updates[q * RHS : (q + 1) * RHS, :], ONE[q])
        RED[me] = (ssep[...] - gathered).astype(BF16)

        def spread(k):
            o = across(k)
            return remote(RED.at[me], RED.at[me], rsnd.at[k], rrcv.at[k], (p, o))

        for k in far_first:
            spread(k).start()
        own_sep.wait()
        total = jnp.zeros((RHS, SHARE), F32)
        for group in range(0, PEERS, GROUP):
            sources = [across(k) for k in range(group, group + GROUP)]
            for k, w in zip(range(group, group + GROUP), sources):
                if k:
                    remote(RED.at[w], RED.at[w], rsnd.at[k], rrcv.at[k], pair).wait_recv()
            for w in sources:
                total += dot(RED[w], SS[pl.ds(pl.multiple_of(w * SHARE, SHARE), SHARE), :])
        half = total.astype(BF16)
        for q in range(4):
            ZP[q * RHS : (q + 1) * RHS, :] = dot_t(half, ONE[q])
        PKS[...] = ZP[...].T.astype(BF16)
        to_owners(PKS, PKR, 6, x, False)
        sep_out[...] = total
        for copy in own_lower:
            copy.wait()
        if x == 0:
            ship_ua.wait_recv()
        several(PKR, PEERS - 1, 6).wait()
        picked = turned(PKR)
        for f in range(2):
            back = dot(picked[f * RHS : (f + 1) * RHS, :], LW[f, 0].reshape(SHARE, LEAF))
            back += dot(picked[(2 + f) * RHS : (3 + f) * RHS, :], LW[f, 1].reshape(SHARE, LEAF))
            leaf_out[f] = swept[f] - back
        for k in range(1, PEERS):
            spread(k).wait_send()

    @pl.when(is0)
    def _core0():
        @pl.when(first)
        def _():
            for copy in ship_da:
                copy.start()

        send_cp.start()
        send_src.start()
        give_a()
        send_targets()
        @pl.when(second)
        def _():
            for g in range(2):
                rows = slice(g * HALF, (g + 1) * HALF)
                side_wave(g).wait_recv()
                loaded = src[1, rows, :] + CP[0, 1:2, :] * T[1, rows, :].astype(F32)
                DA[1, rows, :] = dot(loaded.astype(BF16), A[0, 1]).astype(BF16)
                ship_middle(g).start()
            give_front(1)

        got_cp.wait_recv()
        for x in range(2):
            CT[x] = CP[x].T
        for f in range(2):
            got_a[f].wait_recv()

        @pl.when(c > DIRECT)
        def _():
            for f in range(2):

                @pl.loop(0, 4)
                def _(b):
                    rows = pl.ds(pl.multiple_of(b * 256, 256), 256)
                    left = (A[0, f, rows, :].astype(F32) * CP[1, f : f + 1, :]).astype(BF16)
                    PP[f, rows, :] = (dot(left, A[1, f]) * CT[0, rows, f : f + 1]).astype(BF16)
                    to_pair(PP.at[f, rows], PP.at[f, rows], S_P + f).start()

        for f in range(2):

            @pl.loop(0, 4)
            def _(b):
                rows = pl.ds(pl.multiple_of(b * 256, 256), 256)
                base = jnp.where(last, PP[f, rows, :].astype(F32), A[1, f, rows, :].astype(F32))
                left = (base * CP[0, f + 2 : f + 3, :]).astype(BF16)
                scale = jnp.where(last, 1.0, CT[1, rows, f + 2 : f + 3])
                extra = jnp.where(last, CT[0, rows, f : f + 1], 0.0)
                full = dot(left, A[0, f]) * scale + extra * A[0, f, rows, :].astype(F32)
                QQ[f, rows, :] = full.astype(BF16)
                to_pair(QQ.at[f, rows], QQ.at[f, rows], S_Q + f).start()

        send_lift.start()
        own_sep.start()
        for copy in own_lower:
            copy.start()
        build_maps()
        separator(0, UA)
        for copy in (send_cp, send_src, *send_a, send_lift, *ship_q):
            copy.wait_send()

        @pl.when(c > DIRECT)
        def _():
            for copy in ship_p:
                copy.wait_send()

        @pl.when(first)
        def _():
            for copy in ship_da:
                copy.wait_send()

        @pl.when(second)
        def _():
            for g in range(2):
                ship_middle(g).wait_send()

    @pl.when(is1)
    def _core1():
        send_cp.start()
        give_a()
        send_targets()
        own_sep.start()
        own_lift.start()
        for copy in own_lower:
            copy.start()

        below = (p + 2, me)
        above = (p - 2, me)

        def down_wave(f, g, cols=slice(None)):
            rows, k = half_rows(g), 2 * f + g
            return remote(TS.at[f, rows, cols], T.at[f, rows, cols], dsnd.at[k], drcv.at[k], below)

        def up_wave(f, g, cols=slice(None)):
            rows, k = half_rows(g), 2 * f + g
            return remote(US.at[f, rows, cols], U.at[f, rows, cols], usnd.at[k], urcv.at[k], above)

        def send_down(f, g, cols):
            down_wave(f, g, cols).start()

        def send_up(f, g, cols):
            up_wave(f, g, cols).start()

        def half_rows(g):
            return pl.ds(pl.multiple_of(g * HALF, HALF), HALF)

        def coupled(x, f, k):
            return CP[x, pl.ds(f + k, 1), :]

        def each_wave(act):
            for w in range(WAVES):
                act(w // 2, w % 2)

        def waves(ready, left_of, weight, extra, keep, half, copy_of, begin=0, end=WAVES):
            def turn(i, _):
                w = i
                g = lax.rem(w, 2)
                f = w // 2
                rows = half_rows(g)

                ready(f, g)
                left = left_of(f, rows)
                parts = [slice(j * CHUNK, (j + 1) * CHUNK) for j in range(CHUNKS)]
                outs = []
                for cols in parts:
                    out = dot(left, weight[f, :, cols])
                    outs.append(out if extra is None else out + extra[f, rows, cols])
                for cols, out in zip(parts, outs):
                    half[f, rows, cols] = out.astype(BF16)
                    if copy_of is not None:
                        copy_of(f, g, cols)

                for cols, out in zip(parts, outs):
                    keep[f, rows, cols] = out
                return 0

            lax.fori_loop(begin, end, turn, 0)

        def left_of_middle(f, rows):
            loaded = src[f, rows, :] + coupled(1, f, 0) * DA[f, rows, :].astype(F32)
            return loaded.astype(BF16)

        got_cp.wait_recv()

        @pl.when(first)
        def _():
            T[...] = jnp.zeros_like(T)

            def ready(f, g):
                @pl.when(g == 0)
                def _():
                    to_pair(DA.at[f], DA.at[f], S_DA + f).wait_recv()

            def send_first(f, g, cols):
                @pl.when(f == 1)
                def _():
                    side_wave(g, cols).start()

                send_down(f, g, cols)

            waves(ready, left_of_middle, A.at[1], None, DB, TS, send_first)
            send_src.wait_recv()
            for f in range(2):
                got_a[f].wait_recv()

        @pl.when(jnp.logical_and(c > 0, c <= DIRECT))
        def _():
            def ready(f, g):
                @pl.when(f + g == 0)
                def _():
                    send_src.wait_recv()

                @pl.when(g == 0)
                def _():
                    to_pair(A.at[core, f], A.at[1 - core, f], S_A + f).wait_recv()

                down_wave(f, g).wait_recv()

            def left_of(f, rows):
                loaded = SL[f, rows, :] + coupled(0, f, 0) * T[f, rows, :].astype(F32)
                middle = dot(loaded.astype(BF16), A[0, f])
                loaded = src[f, rows, :] + coupled(1, f, 0) * middle.astype(BF16).astype(F32)
                return loaded.astype(BF16)

            @pl.when(second)
            def _():
                waves(ready, left_of, A.at[1], None, DB, TS, send_down, 0, 2)

                def ready_middle(f, g):
                    to_pair(DA.at[1, half_rows(g)], DA.at[1, half_rows(g)], S_DA + g).wait_recv()

                waves(ready_middle, left_of_middle, A.at[1], None, DB, TS, send_down, 2, 4)
                got_a[1].wait_recv()
                for g in range(2):
                    down_wave(1, g).wait_recv()

            @pl.when(c > 1)
            def _():
                waves(ready, left_of, A.at[1], None, DB, TS, send_down)


        @pl.when(c <= DIRECT)
        def _():
            build_maps()

        @pl.when(c > DIRECT)
        def _():
            send_src.wait_recv()
            for f in range(2):
                got_a[f].wait_recv()

            def alone(f, _):
                middle = dot(SL[f].astype(BF16), A[0, f])
                loaded = src[f] + coupled(1, f, 0) * middle.astype(BF16).astype(F32)
                out = dot(loaded.astype(BF16), A[1, f])
                DB[f] = out
                E[f] = out

                @pl.when(last)
                def _():
                    loaded = SL[f] + coupled(0, f, 2) * out.astype(BF16).astype(F32)
                    E[f] = dot(loaded.astype(BF16), A[0, f])

                return 0

            lax.fori_loop(0, 2, alone, 0)
            build_maps()

            def sweep(ship, weight, keep, half, copy_of):
                def ready(f, g):
                    @pl.when(g == 0)
                    def _():
                        to_pair(weight.at[f], weight.at[f], ship + f).wait_recv()

                    down_wave(f, g).wait_recv()

                waves(ready, lambda f, rows: T[f, rows, :], weight, E, keep, half, copy_of)

            @pl.when(c < LAST)
            def _():
                sweep(S_P, PP, DB, TS, send_down)

            @pl.when(last)
            def _():
                sweep(S_Q, QQ, UA, US, send_up)
                for f in range(2):
                    ship_p[f].wait_recv()

        @pl.when(c < LAST)
        def _():
            def before(f, _):
                loaded = (
                    SL[f]
                    + coupled(0, f, 0) * T[f].astype(F32)
                    + coupled(0, f, 2) * DB[f].astype(BF16).astype(F32)
                )
                G[f] = dot(loaded.astype(BF16), A[0, f])
                return 0

            lax.fori_loop(0, 2, before, 0)

            for f in range(2):
                ship_q[f].wait_recv()

            def ready(f, g):
                up_wave(f, g).wait_recv()

            def left_of(f, rows):
                return U[f, rows, :]

            @pl.when(c > 0)
            def _():
                waves(ready, left_of, QQ, G, UA, US, send_up)

        def lifted(x, update_of):
            for f in range(2):
                Z[f * RHS : (f + 1) * RHS, :] = update_of(f)
            rows = Z[0 : 2 * RHS, :].T.reshape(PEERS, 2, ROWS, 2 * RHS)
            packed = jnp.concatenate([rows[:, 0], rows[:, 1]], axis=-1)
            UPS[x] = packed.reshape(SHARE, 128).astype(BF16)
            to_owners(UPS.at[x], UPR, 4 + x, x, x == 0)

        send_lift.wait_recv()
        own_lift.wait()

        def own_rest(f, _):
            loaded = coupled(1, f, 2) * U[f].astype(F32)
            UB[f] = DB[f] + dot(loaded.astype(BF16), A[1, f])
            return 0

        @pl.when(first)
        def _():
            CT[1] = CP[1].T
            for f in range(2):

                @pl.loop(0, 4)
                def _(b):
                    rows = pl.ds(pl.multiple_of(b * 256, 256), 256)
                    QL[f, rows, :] = dot(QQ[f, rows, :], LL[0, f]).astype(BF16)
                    both = dot(A[1, f, rows, :], LL[1, f]) * CT[1, rows, f + 2 : f + 3]
                    NL[f, rows, :] = both.astype(BF16)

                GL[f] = dot(G[f].astype(BF16), LL[0, f])
                DL[f] = dot(DB[f].astype(BF16), LL[1, f])

            def from_wave(f):
                for g in range(2):
                    up_wave(f, g).wait_recv()
                return GL[f] + dot(U[f], QL[f])

            lifted(0, from_wave)
            lifted(1, lambda f: DL[f] + dot(U[f], NL[f]))

            def last_solve(f, _):
                UA[f] = G[f] + dot(U[f], QQ[f])
                return 0

            lax.fori_loop(0, 2, last_solve, 0)
            ship_ua.start()
            lax.fori_loop(0, 2, own_rest, 0)

        @pl.when(c > 0)
        def _():
            lifted(0, lambda f: dot(US[f], LL[0, f]))
            ship_ua.start()

            @pl.when(last)
            def _():
                def rest(f, _):
                    UB[f] = DB[f] + dot(T[f], PP[f])
                    return 0

                lax.fori_loop(0, 2, rest, 0)

            @pl.when(c < LAST)
            def _():
                lax.fori_loop(0, 2, own_rest, 0)

            lifted(1, lambda f: dot(UB[f].astype(BF16), LL[1, f]))

        separator(1, UB)

        for copy in (send_cp, *send_a, ship_ua):
            copy.wait_send()
        several(UPR, PEERS, 4).wait_send()
        several(UPR, PEERS - 1, 5).wait_send()

        @pl.when(c < LAST)
        def _():
            each_wave(lambda f, g: down_wave(f, g).wait_send())

        @pl.when(first)
        def _():
            for g in range(2):
                side_wave(g).wait_send()

        @pl.when(c > 0)
        def _():
            each_wave(lambda f, g: up_wave(f, g).wait_send())


def hand_over(leaf, sep, leaf_out, sep_out, sem):
    copies = [
        pltpu.make_async_copy(leaf, leaf_out, sem.at[0]),
        pltpu.make_async_copy(sep, sep_out, sem.at[1]),
    ]
    for copy in copies:
        copy.start()
    for copy in copies:
        copy.wait()


def local(source_leaf, source_sep, leaf_inverse, lift, lower, sep_inverse, parent_map, couple_down, couple_up):
    vmem = pl.BlockSpec(memory_space=pltpu.VMEM)
    hbm = pl.BlockSpec(memory_space=pl.ANY)
    trace = (2, RHS, LEAF)
    leaf, sep = pl.pallas_call(
        kernel,
        out_shape=(pltpu.VMEM(trace, F32), pltpu.VMEM((RHS, SHARE), F32)),
        in_specs=[vmem, vmem, hbm, hbm, hbm, hbm, vmem, vmem, vmem],
        out_specs=(vmem, vmem),
        scratch_shapes=[
            pltpu.VMEM((2, 2, LEAF, LEAF), BF16),
            pltpu.VMEM((2, LEAF, LEAF), BF16),
            pltpu.VMEM((2, LEAF, LEAF), BF16),
            pltpu.VMEM((2, 2, LEAF, UPD), BF16),
            pltpu.VMEM((2, 2, PEERS, ROWS, LEAF), BF16),
            pltpu.VMEM((PEERS * SHARE, SHARE), BF16),
            pltpu.VMEM(trace, F32),
            pltpu.VMEM((2, 8, LEAF), F32),
            pltpu.VMEM((2, LEAF, 8), F32),
            *[pltpu.VMEM(trace, BF16) for _ in range(5)],
            *[pltpu.VMEM(trace, F32) for _ in range(5)],
            *[pltpu.VMEM((2, LEAF, UPD), BF16) for _ in range(2)],
            *[pltpu.VMEM((2, RHS, UPD), F32) for _ in range(2)],
            pltpu.VMEM((128, UPD), F32),
            pltpu.VMEM((128, SHARE), F32),
            pltpu.VMEM((SHARE, 128), F32),
            pltpu.VMEM((PEERS, ROWS, 128), F32),
            pltpu.VMEM((2, SHARE, 128), BF16),
            pltpu.VMEM((PEERS, ROWS, 128), BF16),
            pltpu.VMEM((4, SHARE, SHARE), BF16),
            pltpu.VMEM((PEERS, RHS, SHARE), BF16),
            pltpu.VMEM((SHARE, 128), BF16),
            pltpu.VMEM((PEERS, ROWS, 128), BF16),
            pltpu.SemaphoreType.DMA((8,)),
            pltpu.SemaphoreType.DMA((12,)),
            pltpu.SemaphoreType.DMA((12,)),
            *[pltpu.SemaphoreType.DMA((WAVES,)) for _ in range(4)],
            pltpu.SemaphoreType.DMA((8,)),
            pltpu.SemaphoreType.DMA((8,)),
            pltpu.SemaphoreType.DMA((PEERS,)),
            pltpu.SemaphoreType.DMA((PEERS,)),
        ],
        compiler_params=pltpu.CompilerParams(
            collective_id=0, has_side_effects=True, vmem_limit_bytes=56 * 1024 * 1024
        ),
        name="sweep",
    )(
        source_leaf[0], source_sep[0], leaf_inverse[0], lift[0], lower.reshape(2, PEERS, 2, ROWS, LEAF),
        sep_inverse[0], parent_map[0], couple_down[0], couple_up[0],
    )
    leaf, sep = pl.pallas_call(
        hand_over,
        out_shape=(jax.ShapeDtypeStruct(trace, F32), jax.ShapeDtypeStruct((RHS, SHARE), F32)),
        in_specs=[hbm, hbm],
        out_specs=(hbm, hbm),
        scratch_shapes=[pltpu.SemaphoreType.DMA((2,))],
        name="hand_over",
    )(
        pltpu.with_memory_space_constraint(leaf, pltpu.VMEM),
        pltpu.with_memory_space_constraint(sep, pltpu.VMEM),
    )
    return leaf[None], sep[None]


def solution(mesh):
    return jax.shard_map(
        local,
        mesh=mesh,
        in_specs=(
            P("panel", "front", None, None),
            P("panel", None, "front"),
            P("panel", "front", None, None),
            P("panel", "front", None, None),
            P("panel", "front", None, None),
            P("panel", None, "front"),
            P("panel", "front", None),
            P("panel", "front", None),
            P("panel", "front", None),
        ),
        out_specs=(P("panel", "front", None, None), P("panel", None, "front")),
        check_vma=False,
    )
```

```python
import jax
import jax.numpy as jnp
from jax import lax
from jax.experimental import pallas as pl
from jax.experimental.pallas import tpu as pltpu
from jax.sharding import PartitionSpec as P

MESH = pl.DeviceIdType.MESH
F32 = jnp.float32
BF16 = jnp.bfloat16
LEAF = 1024
UPD = 512
SHARE = 256
RHS = 32
ROWS = 16
GROUP = 4
PEERS = 16
LAST = 7
DIRECT = 3
HALF = 16
WAVES = 4
CHUNK = 512
CHUNKS = LEAF // CHUNK

S_CP, S_SRC, S_A, S_LIFT, S_P, S_Q, S_UA, S_DA = 0, 1, 2, 4, 5, 7, 9, 10


def dot(a, b):
    return jnp.dot(a, b, preferred_element_type=F32)


def dot_t(a, b):
    return lax.dot_general(a, b, (((1,), (1,)), ((), ())), preferred_element_type=F32)


def kernel(
    src, ssep, inv, lift, lower, sepinv, pm, cd, cu,
    leaf_out, sep_out,
    A, PP, QQ, LL, LW, SS, SL, CP, CT,
    T, U, TS, US, DA, E, DB, G, UA, UB,
    NL, QL, DL, GL, Z, ZP, PMS, PMR, UPS, UPR, ONE, RED, PKS, PKR,
    lsem, ps, pr, dsnd, drcv, usnd, urcv, osnd, orcv, rsnd, rrcv,
):
    p = lax.axis_index("panel")
    me = lax.axis_index("front")
    core = lax.rem(p, 2)
    c = p // 2
    pair = (p + 1 - 2 * core, me)
    is0 = core == 0
    is1 = core == 1
    first = c == 0
    second = c == 1
    last = c == LAST
    def remote(s, d, ss, rs, dev):
        return pltpu.make_async_remote_copy(
            src_ref=s, dst_ref=d, send_sem=ss, recv_sem=rs, device_id=dev, device_id_type=MESH
        )

    def to_pair(s, d, i):
        return remote(s, d, ps.at[i], pr.at[i], pair)

    own = [pltpu.make_async_copy(inv.at[f], A.at[core, f], lsem.at[f]) for f in range(2)]
    own_lift = pltpu.make_async_copy(lift, LL.at[1], lsem.at[2])
    own_lower = [
        pltpu.make_async_copy(lower.at[f, :, h], LW.at[f, h], lsem.at[4 + 2 * f + h])
        for f in range(2)
        for h in range(2)
    ]
    own_sep = pltpu.make_async_copy(sepinv, SS, lsem.at[3])
    for copy in own:
        copy.start()

    barrier = pltpu.get_barrier_semaphore()

    def signal(dev):
        pl.semaphore_signal(barrier, inc=1, device_id=dev, device_id_type=MESH)

    @pl.when(is1)
    def _():
        @pl.when(c < LAST)
        def _():
            signal((p + 2, me))

        @pl.when(c > 0)
        def _():
            signal((p - 2, me))

        signal(pair)

    @pl.when(jnp.logical_and(is0, second))
    def _():
        signal((p - 1, me))

    def greet(k, _):
        o = lax.rem(me + k, PEERS)

        @pl.when(k > 0)
        def _():
            signal((p, o))

        @pl.when(is0)
        def _():
            signal((p + 1, o))

        return 0

    lax.fori_loop(0, PEERS, greet, 0)
    CP[core, 0:2, :] = cd[...]
    CP[core, 2:4, :] = cu[...]
    Z[...] = jnp.zeros_like(Z)
    Z[0:2, :] = pm[...].astype(F32)
    Z[2:4, :] = pm[...].astype(F32)
    targets = Z[...].T.reshape(PEERS, 2, ROWS, 128)
    lane = lax.broadcasted_iota(jnp.int32, (PEERS, ROWS, 128), 2)
    PMS[...] = jnp.where(lane < 2, targets[:, 0], targets[:, 1]).reshape(PEERS * ROWS, 128)

    @pl.when(jnp.logical_and(is0, first))
    def _():
        for f in range(2):
            own[f].wait()
            DA[f] = dot(src[f].astype(BF16), A[0, f]).astype(BF16)

    ends = 1 + jnp.where(last, 0, 1)
    far = PEERS + ends
    pl.semaphore_wait(barrier, PEERS - 1 + jnp.where(is1, far, 1))

    send_a = [to_pair(A.at[core, f], A.at[core, f], S_A + f) for f in range(2)]
    got_a = [to_pair(A.at[core, f], A.at[1 - core, f], S_A + f) for f in range(2)]

    def give_front(f):
        for half in range(2):
            rows = pl.ds(half * 512, 512)
            to_pair(A.at[core, f, rows], A.at[core, f, rows], S_A + f).start()

    def give_a():
        for f in range(2):

            @pl.when(jnp.logical_or(is1, c > 0))
            def _():
                own[f].wait()

            if f == 0:
                give_front(0)
            else:

                @pl.when(jnp.logical_or(is1, jnp.logical_not(second)))
                def _():
                    give_front(1)

    send_cp = to_pair(CP.at[core], CP.at[core], S_CP)
    got_cp = to_pair(CP.at[core], CP.at[1 - core], S_CP)
    send_src = to_pair(src, SL, S_SRC)
    send_lift = to_pair(lift, LL.at[0], S_LIFT)
    ship_p = [to_pair(PP.at[f], PP.at[f], S_P + f) for f in range(2)]
    ship_q = [to_pair(QQ.at[f], QQ.at[f], S_Q + f) for f in range(2)]
    ship_ua = to_pair(UA, UA, S_UA)
    ship_da = [to_pair(DA.at[f], DA.at[f], S_DA + f) for f in range(2)]
    def side_wave(g, cols=slice(None)):
        rows = pl.ds(pl.multiple_of(g * HALF, HALF), HALF)
        return remote(TS.at[1, rows, cols], T.at[1, rows, cols], osnd.at[g], orcv.at[g], (p + 1, me))

    def ship_middle(g):
        rows = pl.ds(g * HALF, HALF)
        return to_pair(DA.at[1, rows], DA.at[1, rows], S_DA + g)

    def part(k):
        return pl.ds(pl.multiple_of(k * ROWS, ROWS), ROWS)

    def flipped(v, bits):
        return (v, v + 1 - 2 * lax.rem(v, 2), lax.rem(v + 2, 4), 3 - v)[bits]

    def across(k):
        return 4 * flipped(me // 4, k // 4) + flipped(lax.rem(me, 4), k % 4)

    far_first = range(PEERS - 1, 0, -1)

    def to_owners(out, into, lane, target, to_self):
        for k in (*far_first, *([0] if to_self else [])):
            o = across(k)
            remote(
                out.at[part(o)], into.at[me], osnd.at[lane], orcv.at[lane], (2 * c + target, o)
            ).start()
        if not to_self:
            into[me] = out[part(me), :]

    def several(ref, n, lane):
        some = ref.at[pl.ds(0, n)]
        return remote(some, some, osnd.at[lane], orcv.at[lane], pair)

    def send_targets():
        to_owners(PMS, PMR, 3, core, False)

    def build_maps():
        several(PMR, PEERS - 1, 3).wait()
        table = PMR[...].reshape(SHARE, 128)
        column = (lax.broadcasted_iota(jnp.int32, (SHARE, SHARE), 1) + me * SHARE).astype(F32)
        for q in range(4):
            ONE[q] = jnp.where(table[:, q : q + 1] == column, 1.0, 0.0).astype(BF16)

    def turned(ref):
        return ref[...].astype(F32).reshape(SHARE, 128).T.astype(BF16)

    def separator(x, swept):
        several(UPR, PEERS - x, 4 + x).wait_recv()
        updates = turned(UPR)
        gathered = jnp.zeros((RHS, SHARE), F32)
        for q in range(4):
            gathered += dot(updates[q * RHS : (q + 1) * RHS, :], ONE[q])
        RED[me] = (ssep[...] - gathered).astype(BF16)

        def spread(k):
            o = across(k)
            return remote(RED.at[me], RED.at[me], rsnd.at[k], rrcv.at[k], (p, o))

        for k in far_first:
            spread(k).start()
        own_sep.wait()
        total = jnp.zeros((RHS, SHARE), F32)
        for group in range(0, PEERS, GROUP):
            sources = [across(k) for k in range(group, group + GROUP)]
            for k, w in zip(range(group, group + GROUP), sources):
                if k:
                    remote(RED.at[w], RED.at[w], rsnd.at[k], rrcv.at[k], pair).wait_recv()
            for w in sources:
                total += dot(RED[w], SS[pl.ds(pl.multiple_of(w * SHARE, SHARE), SHARE), :])
        half = total.astype(BF16)
        for q in range(4):
            ZP[q * RHS : (q + 1) * RHS, :] = dot_t(half, ONE[q])
        PKS[...] = ZP[...].T.astype(BF16)
        to_owners(PKS, PKR, 6, x, False)
        sep_out[...] = total
        for copy in own_lower:
            copy.wait()
        if x == 0:
            ship_ua.wait_recv()
        several(PKR, PEERS - 1, 6).wait()
        picked = turned(PKR)
        for f in range(2):
            back = dot(picked[f * RHS : (f + 1) * RHS, :], LW[f, 0].reshape(SHARE, LEAF))
            back += dot(picked[(2 + f) * RHS : (3 + f) * RHS, :], LW[f, 1].reshape(SHARE, LEAF))
            leaf_out[f] = swept[f] - back
        for k in range(1, PEERS):
            spread(k).wait_send()

    @pl.when(is0)
    def _core0():
        @pl.when(first)
        def _():
            for copy in ship_da:
                copy.start()

        send_cp.start()
        send_src.start()
        give_a()
        send_targets()
        @pl.when(second)
        def _():
            for g in range(2):
                rows = slice(g * HALF, (g + 1) * HALF)
                side_wave(g).wait_recv()
                loaded = src[1, rows, :] + CP[0, 1:2, :] * T[1, rows, :].astype(F32)
                DA[1, rows, :] = dot(loaded.astype(BF16), A[0, 1]).astype(BF16)
                ship_middle(g).start()
            give_front(1)

        got_cp.wait_recv()
        for x in range(2):
            CT[x] = CP[x].T
        for f in range(2):
            got_a[f].wait_recv()

        @pl.when(c > DIRECT)
        def _():
            for f in range(2):

                @pl.loop(0, 4)
                def _(b):
                    rows = pl.ds(pl.multiple_of(b * 256, 256), 256)
                    left = (A[0, f, rows, :].astype(F32) * CP[1, f : f + 1, :]).astype(BF16)
                    PP[f, rows, :] = (dot(left, A[1, f]) * CT[0, rows, f : f + 1]).astype(BF16)
                    to_pair(PP.at[f, rows], PP.at[f, rows], S_P + f).start()

        for f in range(2):

            @pl.loop(0, 4)
            def _(b):
                rows = pl.ds(pl.multiple_of(b * 256, 256), 256)
                base = jnp.where(last, PP[f, rows, :].astype(F32), A[1, f, rows, :].astype(F32))
                left = (base * CP[0, f + 2 : f + 3, :]).astype(BF16)
                scale = jnp.where(last, 1.0, CT[1, rows, f + 2 : f + 3])
                extra = jnp.where(last, CT[0, rows, f : f + 1], 0.0)
                full = dot(left, A[0, f]) * scale + extra * A[0, f, rows, :].astype(F32)
                QQ[f, rows, :] = full.astype(BF16)
                to_pair(QQ.at[f, rows], QQ.at[f, rows], S_Q + f).start()

        send_lift.start()
        own_sep.start()
        for copy in own_lower:
            copy.start()
        build_maps()
        separator(0, UA)
        for copy in (send_cp, send_src, *send_a, send_lift, *ship_q):
            copy.wait_send()

        @pl.when(c > DIRECT)
        def _():
            for copy in ship_p:
                copy.wait_send()

        @pl.when(first)
        def _():
            for copy in ship_da:
                copy.wait_send()

        @pl.when(second)
        def _():
            for g in range(2):
                ship_middle(g).wait_send()

    @pl.when(is1)
    def _core1():
        send_cp.start()
        for copy in own:
            copy.wait()

        @pl.when(c > DIRECT)
        def _():
            give_front(0)
            give_front(1)

        send_targets()
        own_sep.start()
        own_lift.start()
        for copy in own_lower:
            copy.start()

        below = (p + 2, me)
        above = (p - 2, me)

        def down_wave(f, g, cols=slice(None)):
            rows, k = half_rows(g), 2 * f + g
            return remote(TS.at[f, rows, cols], T.at[f, rows, cols], dsnd.at[k], drcv.at[k], below)

        def up_wave(f, g, cols=slice(None)):
            rows, k = half_rows(g), 2 * f + g
            return remote(US.at[f, rows, cols], U.at[f, rows, cols], usnd.at[k], urcv.at[k], above)

        def send_down(f, g, cols):
            down_wave(f, g, cols).start()

        def send_up(f, g, cols):
            up_wave(f, g, cols).start()

        def half_rows(g):
            return pl.ds(pl.multiple_of(g * HALF, HALF), HALF)

        def coupled(x, f, k):
            return CP[x, pl.ds(f + k, 1), :]

        def each_wave(act):
            for w in range(WAVES):
                act(w // 2, w % 2)

        def waves(ready, left_of, weight, extra, keep, half, copy_of, begin=0, end=WAVES):
            def turn(i, _):
                w = i
                g = lax.rem(w, 2)
                f = w // 2
                rows = half_rows(g)

                ready(f, g)
                left = left_of(f, rows)
                parts = [slice(j * CHUNK, (j + 1) * CHUNK) for j in range(CHUNKS)]
                outs = []
                for cols in parts:
                    out = dot(left, weight[f, :, cols])
                    outs.append(out if extra is None else out + extra[f, rows, cols])
                for cols, out in zip(parts, outs):
                    half[f, rows, cols] = out.astype(BF16)
                    if copy_of is not None:
                        copy_of(f, g, cols)

                for cols, out in zip(parts, outs):
                    keep[f, rows, cols] = out
                return 0

            lax.fori_loop(begin, end, turn, 0)

        def left_of_middle(f, rows):
            loaded = src[f, rows, :] + coupled(1, f, 0) * DA[f, rows, :].astype(F32)
            return loaded.astype(BF16)

        got_cp.wait_recv()

        @pl.when(first)
        def _():
            T[...] = jnp.zeros_like(T)

            def ready(f, g):
                @pl.when(g == 0)
                def _():
                    to_pair(DA.at[f], DA.at[f], S_DA + f).wait_recv()

            def send_first(f, g, cols):
                @pl.when(f == 1)
                def _():
                    side_wave(g, cols).start()

                send_down(f, g, cols)

            waves(ready, left_of_middle, A.at[1], None, DB, TS, send_first)
            send_src.wait_recv()
            for f in range(2):
                got_a[f].wait_recv()

        @pl.when(jnp.logical_and(c > 0, c <= DIRECT))
        def _():
            def ready(f, g):
                @pl.when(f + g == 0)
                def _():
                    send_src.wait_recv()

                @pl.when(g == 0)
                def _():
                    to_pair(A.at[core, f], A.at[1 - core, f], S_A + f).wait_recv()

                down_wave(f, g).wait_recv()

            def left_of(f, rows):
                loaded = SL[f, rows, :] + coupled(0, f, 0) * T[f, rows, :].astype(F32)
                middle = dot(loaded.astype(BF16), A[0, f])
                loaded = src[f, rows, :] + coupled(1, f, 0) * middle.astype(BF16).astype(F32)
                return loaded.astype(BF16)

            @pl.when(second)
            def _():
                waves(ready, left_of, A.at[1], None, DB, TS, send_down, 0, 2)

                def ready_middle(f, g):
                    to_pair(DA.at[1, half_rows(g)], DA.at[1, half_rows(g)], S_DA + g).wait_recv()

                waves(ready_middle, left_of_middle, A.at[1], None, DB, TS, send_down, 2, 4)
                got_a[1].wait_recv()
                for g in range(2):
                    down_wave(1, g).wait_recv()

            @pl.when(c > 1)
            def _():
                waves(ready, left_of, A.at[1], None, DB, TS, send_down)


        @pl.when(c <= DIRECT)
        def _():
            give_front(0)
            give_front(1)
            build_maps()

        @pl.when(c > DIRECT)
        def _():
            send_src.wait_recv()
            for f in range(2):
                got_a[f].wait_recv()

            def alone(f, _):
                middle = dot(SL[f].astype(BF16), A[0, f])
                loaded = src[f] + coupled(1, f, 0) * middle.astype(BF16).astype(F32)
                out = dot(loaded.astype(BF16), A[1, f])
                DB[f] = out
                E[f] = out

                @pl.when(last)
                def _():
                    loaded = SL[f] + coupled(0, f, 2) * out.astype(BF16).astype(F32)
                    E[f] = dot(loaded.astype(BF16), A[0, f])

                return 0

            lax.fori_loop(0, 2, alone, 0)
            build_maps()

            def sweep(ship, weight, keep, half, copy_of):
                def ready(f, g):
                    @pl.when(g == 0)
                    def _():
                        to_pair(weight.at[f], weight.at[f], ship + f).wait_recv()

                    down_wave(f, g).wait_recv()

                waves(ready, lambda f, rows: T[f, rows, :], weight, E, keep, half, copy_of)

            @pl.when(c < LAST)
            def _():
                sweep(S_P, PP, DB, TS, send_down)

            @pl.when(last)
            def _():
                sweep(S_Q, QQ, UA, US, send_up)
                for f in range(2):
                    ship_p[f].wait_recv()

        @pl.when(c < LAST)
        def _():
            def before(f, _):
                loaded = (
                    SL[f]
                    + coupled(0, f, 0) * T[f].astype(F32)
                    + coupled(0, f, 2) * DB[f].astype(BF16).astype(F32)
                )
                G[f] = dot(loaded.astype(BF16), A[0, f])
                return 0

            lax.fori_loop(0, 2, before, 0)

            for f in range(2):
                ship_q[f].wait_recv()

            def ready(f, g):
                up_wave(f, g).wait_recv()

            def left_of(f, rows):
                return U[f, rows, :]

            @pl.when(c > 0)
            def _():
                waves(ready, left_of, QQ, G, UA, US, send_up)

        def lifted(x, update_of):
            for f in range(2):
                Z[f * RHS : (f + 1) * RHS, :] = update_of(f)
            rows = Z[0 : 2 * RHS, :].T.reshape(PEERS, 2, ROWS, 2 * RHS)
            packed = jnp.concatenate([rows[:, 0], rows[:, 1]], axis=-1)
            UPS[x] = packed.reshape(SHARE, 128).astype(BF16)
            to_owners(UPS.at[x], UPR, 4 + x, x, x == 0)

        send_lift.wait_recv()
        own_lift.wait()

        def own_rest(f, _):
            loaded = coupled(1, f, 2) * U[f].astype(F32)
            UB[f] = DB[f] + dot(loaded.astype(BF16), A[1, f])
            return 0

        @pl.when(first)
        def _():
            CT[1] = CP[1].T
            for f in range(2):

                @pl.loop(0, 4)
                def _(b):
                    rows = pl.ds(pl.multiple_of(b * 256, 256), 256)
                    QL[f, rows, :] = dot(QQ[f, rows, :], LL[0, f]).astype(BF16)
                    both = dot(A[1, f, rows, :], LL[1, f]) * CT[1, rows, f + 2 : f + 3]
                    NL[f, rows, :] = both.astype(BF16)

                GL[f] = dot(G[f].astype(BF16), LL[0, f])
                DL[f] = dot(DB[f].astype(BF16), LL[1, f])

            def from_wave(f):
                for g in range(2):
                    up_wave(f, g).wait_recv()
                return GL[f] + dot(U[f], QL[f])

            lifted(0, from_wave)
            lifted(1, lambda f: DL[f] + dot(U[f], NL[f]))

            def last_solve(f, _):
                UA[f] = G[f] + dot(U[f], QQ[f])
                return 0

            lax.fori_loop(0, 2, last_solve, 0)
            ship_ua.start()
            lax.fori_loop(0, 2, own_rest, 0)

        @pl.when(c > 0)
        def _():
            lifted(0, lambda f: dot(US[f], LL[0, f]))
            ship_ua.start()

            @pl.when(last)
            def _():
                def rest(f, _):
                    UB[f] = DB[f] + dot(T[f], PP[f])
                    return 0

                lax.fori_loop(0, 2, rest, 0)

            @pl.when(c < LAST)
            def _():
                lax.fori_loop(0, 2, own_rest, 0)

            lifted(1, lambda f: dot(UB[f].astype(BF16), LL[1, f]))

        separator(1, UB)

        for copy in (send_cp, *send_a, ship_ua):
            copy.wait_send()
        several(UPR, PEERS, 4).wait_send()
        several(UPR, PEERS - 1, 5).wait_send()

        @pl.when(c < LAST)
        def _():
            each_wave(lambda f, g: down_wave(f, g).wait_send())

        @pl.when(first)
        def _():
            for g in range(2):
                side_wave(g).wait_send()

        @pl.when(c > 0)
        def _():
            each_wave(lambda f, g: up_wave(f, g).wait_send())


def hand_over(leaf, sep, leaf_out, sep_out, sem):
    copies = [
        pltpu.make_async_copy(leaf, leaf_out, sem.at[0]),
        pltpu.make_async_copy(sep, sep_out, sem.at[1]),
    ]
    for copy in copies:
        copy.start()
    for copy in copies:
        copy.wait()


def local(source_leaf, source_sep, leaf_inverse, lift, lower, sep_inverse, parent_map, couple_down, couple_up):
    vmem = pl.BlockSpec(memory_space=pltpu.VMEM)
    hbm = pl.BlockSpec(memory_space=pl.ANY)
    trace = (2, RHS, LEAF)
    leaf, sep = pl.pallas_call(
        kernel,
        out_shape=(pltpu.VMEM(trace, F32), pltpu.VMEM((RHS, SHARE), F32)),
        in_specs=[vmem, vmem, hbm, hbm, hbm, hbm, vmem, vmem, vmem],
        out_specs=(vmem, vmem),
        scratch_shapes=[
            pltpu.VMEM((2, 2, LEAF, LEAF), BF16),
            pltpu.VMEM((2, LEAF, LEAF), BF16),
            pltpu.VMEM((2, LEAF, LEAF), BF16),
            pltpu.VMEM((2, 2, LEAF, UPD), BF16),
            pltpu.VMEM((2, 2, PEERS, ROWS, LEAF), BF16),
            pltpu.VMEM((PEERS * SHARE, SHARE), BF16),
            pltpu.VMEM(trace, F32),
            pltpu.VMEM((2, 8, LEAF), F32),
            pltpu.VMEM((2, LEAF, 8), F32),
            *[pltpu.VMEM(trace, BF16) for _ in range(5)],
            *[pltpu.VMEM(trace, F32) for _ in range(5)],
            *[pltpu.VMEM((2, LEAF, UPD), BF16) for _ in range(2)],
            *[pltpu.VMEM((2, RHS, UPD), F32) for _ in range(2)],
            pltpu.VMEM((128, UPD), F32),
            pltpu.VMEM((128, SHARE), F32),
            pltpu.VMEM((SHARE, 128), F32),
            pltpu.VMEM((PEERS, ROWS, 128), F32),
            pltpu.VMEM((2, SHARE, 128), BF16),
            pltpu.VMEM((PEERS, ROWS, 128), BF16),
            pltpu.VMEM((4, SHARE, SHARE), BF16),
            pltpu.VMEM((PEERS, RHS, SHARE), BF16),
            pltpu.VMEM((SHARE, 128), BF16),
            pltpu.VMEM((PEERS, ROWS, 128), BF16),
            pltpu.SemaphoreType.DMA((8,)),
            pltpu.SemaphoreType.DMA((12,)),
            pltpu.SemaphoreType.DMA((12,)),
            *[pltpu.SemaphoreType.DMA((WAVES,)) for _ in range(4)],
            pltpu.SemaphoreType.DMA((8,)),
            pltpu.SemaphoreType.DMA((8,)),
            pltpu.SemaphoreType.DMA((PEERS,)),
            pltpu.SemaphoreType.DMA((PEERS,)),
        ],
        compiler_params=pltpu.CompilerParams(
            collective_id=0, has_side_effects=True, vmem_limit_bytes=56 * 1024 * 1024
        ),
        name="sweep",
    )(
        source_leaf[0], source_sep[0], leaf_inverse[0], lift[0], lower.reshape(2, PEERS, 2, ROWS, LEAF),
        sep_inverse[0], parent_map[0], couple_down[0], couple_up[0],
    )
    leaf, sep = pl.pallas_call(
        hand_over,
        out_shape=(jax.ShapeDtypeStruct(trace, F32), jax.ShapeDtypeStruct((RHS, SHARE), F32)),
        in_specs=[hbm, hbm],
        out_specs=(hbm, hbm),
        scratch_shapes=[pltpu.SemaphoreType.DMA((2,))],
        name="hand_over",
    )(
        pltpu.with_memory_space_constraint(leaf, pltpu.VMEM),
        pltpu.with_memory_space_constraint(sep, pltpu.VMEM),
    )
    return leaf[None], sep[None]


def solution(mesh):
    return jax.shard_map(
        local,
        mesh=mesh,
        in_specs=(
            P("panel", "front", None, None),
            P("panel", None, "front"),
            P("panel", "front", None, None),
            P("panel", "front", None, None),
            P("panel", "front", None, None),
            P("panel", None, "front"),
            P("panel", "front", None),
            P("panel", "front", None),
            P("panel", "front", None),
        ),
        out_specs=(P("panel", "front", None, None), P("panel", None, "front")),
        check_vma=False,
    )
```
